256 devices in a mesh: span: 16 (over x, y), tensor: 16 (over z, core).
Axes of the slice: x: 4, y: 4, z: 8, core: 2. Of those that a mesh axis runs over, the one named last changes fastest.
Arguments:
- tokens: bfloat16 [4096, 4096], P('span', 'tensor'), may hold values from -200 to 200
- retain: float32 [4096], P('span'), may hold values from 0.5 to 1
- norm_gain: float32 [4096], P('tensor'), may hold values from 0.1 to 1.9
- norm_bias: float32 [4096], P('tensor'), may hold values from -2.5 to 2.5
- decay_rate: float32 [16, 4096], P(None, 'tensor'), may hold values from 6.1035156e-05 to 0.0333333333
- ema_angle: float32 [16, 4096], P(None, 'tensor'), may hold values from -0.05 to 0.05
- ema_input: float32 [16, 4096], P(None, 'tensor'), may hold values from -2.4 to 2.4
- ema_output: float32 [2, 16, 4096], P(None, None, 'tensor'), may hold values from -0.25 to 0.25
- ema_skip: float32 [4096], P('tensor'), may hold values from -3 to 3
- shared_weight: bfloat16 [4096, 1024], P('tensor'), may hold values from -0.125 to 0.125
- shared_gain: float32 [1024], replicated, may hold values from 0.1 to 1.9
- output_weight: bfloat16 [1024, 4096], P(None, 'tensor'), may hold values from -0.1875 to 0.1875
Outputs:
- layer_out: bfloat16 [4096, 4096], P('span', 'tensor')
The draws below stay inside these ranges and needn't reach their ends.
All inputs are finite; a program needn't handle non-finite values.
Results may differ from the reference program's by a relative error of at most 0.02.
Values may be sent and summed in bfloat16 or wider, within the bound.
No kernel may reach another device: no remote copies, remote signals or barrier semaphores. Data moves between devices by JAX's collectives and lax.ppermute only.
A program may use at most 128 MiB of HBM per device.

```python
import jax
import jax.numpy as jnp
from jax import lax

D = 4096
NDIM = 16
Z = 1024
GROUP = 64
BLOCK = 64
STREAM_LENGTH = 4096
N_TENSOR = 16


def draw_tokens(key, part):
    random_seed_list = jax.random.split(jax.random.fold_in(key, 11), 3)
    element_ordinal = jnp.arange(STREAM_LENGTH).astype(jnp.float32) / STREAM_LENGTH
    column_scale = jnp.exp(jax.random.uniform(random_seed_list[0], (D,), minval=0.0, maxval=jnp.log(10.0)))
    start_offset = jnp.clip(jax.random.normal(random_seed_list[1], (D,)), -3.0, 3.0) * 0.7
    growth = 1.0 + 2.0 * element_ordinal
    jitter = jnp.clip(jax.random.normal(random_seed_list[2], (STREAM_LENGTH, D)), -6.0, 6.0)
    values = growth[:, None] * column_scale[None] * (start_offset[None] + jitter)
    return jnp.clip(values, -200.0, 200.0).astype(jnp.bfloat16)


def draw_retain(key, part):
    random_seed_list = jax.random.split(jax.random.fold_in(key, 23), 2)
    peak_spot_index = jax.random.permutation(random_seed_list[0], STREAM_LENGTH)[:8]
    levels = jax.random.uniform(random_seed_list[1], (8,), minval=0.5, maxval=0.7)
    levels = levels.at[0].set(0.5)
    element_ordinal = jnp.arange(STREAM_LENGTH)
    agreeing_outcome = element_ordinal[:, None] == peak_spot_index[None]
    factor = jnp.min(jnp.where(agreeing_outcome, levels[None], 1.0), axis=1)
    return factor.astype(jnp.float32)


def ema_rates(key):
    random_seed_list = jax.random.split(jax.random.fold_in(key, 37), 3)
    chooser = jax.random.uniform(random_seed_list[0], (NDIM, D))
    fast_rate = jnp.exp(jax.random.uniform(random_seed_list[1], (NDIM, D), minval=jnp.log(1.0 / 50), maxval=jnp.log(1.0 / 30)))
    fast_share = 0.25
    slow_top = 4.0
    slow_rate = jnp.exp(jax.random.uniform(random_seed_list[2], (NDIM, D), minval=jnp.log(0.25 / STREAM_LENGTH), maxval=jnp.log(slow_top / STREAM_LENGTH)))
    return jnp.where(chooser < fast_share, fast_rate, slow_rate)


def channel_sign(key):
    flips = jax.random.randint(jax.random.fold_in(key, 53), (D,), 0, 2)
    return (2 * flips - 1).astype(jnp.float32)


def draw_decay_rate(key, part):
    return ema_rates(key).astype(jnp.float32)


def draw_ema_angle(key, part):
    reach = 1.0
    turn = jax.random.uniform(jax.random.fold_in(key, 41), (NDIM, D), minval=-reach, maxval=reach)
    return (ema_rates(key) * turn).astype(jnp.float32)


def draw_ema_input(key, part):
    low, high = (1.0, 2.0)
    size_part = jax.random.uniform(jax.random.fold_in(key, 61), (NDIM, D), minval=low, maxval=high)
    return (channel_sign(key)[None] * size_part).astype(jnp.float32)


def draw_ema_output(key, part):
    random_seed_list = jax.random.split(jax.random.fold_in(key, 67), 2)
    low, high = (0.1, 0.2)
    real_part = channel_sign(key)[None] * jax.random.uniform(random_seed_list[0], (NDIM, D), minval=low, maxval=high)
    imag_part = jax.random.uniform(random_seed_list[1], (NDIM, D), minval=-0.1, maxval=0.1)
    return jnp.stack([real_part, imag_part]).astype(jnp.float32)


def draw_norm_bias(key, part):
    random_seed_list = jax.random.split(jax.random.fold_in(key, 71), 2)
    low, high = (1.0, 2.0)
    flips = jax.random.randint(random_seed_list[0], (D,), 0, 2)
    size_part = jax.random.uniform(random_seed_list[1], (D,), minval=low, maxval=high)
    return ((2 * flips - 1).astype(jnp.float32) * size_part).astype(jnp.float32)


def strengthened(values, key, source, target, shards_of, factor):
    def block_of(axis_at):
        return (jnp.arange(values.shape[axis_at]) // (values.shape[axis_at] // shards_of)).reshape((-1,) + (1,) * (values.ndim - 1 - axis_at))

    one_side = jax.random.permutation(key, shards_of)[block_of(target)]
    other_side = (block_of(target) + shards_of // 2) % shards_of
    return jnp.where((block_of(source) == one_side) | (block_of(source) == other_side), factor * values, values)


def level_of(key, shape, cuts, smallest, largest):
    def one(position, parts):
        draws = jax.random.uniform(jax.random.fold_in(jax.random.fold_in(key, 6), position), (parts,), jnp.float32, smallest / len(cuts), largest / len(cuts))
        return jnp.repeat(jnp.exp(draws), shape[position] // parts).reshape((-1,) + (1,) * (len(shape) - position - 1))

    loudness = one(*cuts[0])
    for cut in cuts[1:]:
        loudness = loudness * one(*cut)
    return loudness


def scatter_about(stream_key, extent, scale, most, pieces=(), kind=jnp.bfloat16):
    array = jax.random.normal(stream_key, extent, jnp.float32) * scale
    if len(pieces) > 0:
        array = level_of(stream_key, extent, pieces, -0.22, 0.18) * array
    return jnp.clip(array, min=-most, max=most).astype(kind)


def heavy_noise(own_key, extent, scale, bound, cuts, heavy, held_as=jnp.bfloat16):
    entries = scale * jax.random.normal(own_key, extent, jnp.float32)
    if cuts:
        entries = entries * level_of(own_key, extent, cuts, -0.22, 0.18)
    return jnp.clip(strengthened(entries, jax.random.fold_in(own_key, 3), *heavy), -bound, bound).astype(held_as)


def setup_inputs(seed: int = 0) -> dict:
    streams_of = jax.random.split(jax.random.key(seed), 13)
    return {
        "tokens": draw_tokens(jax.random.fold_in(streams_of[12], 71), 0),
        "retain": draw_retain(jax.random.fold_in(streams_of[12], 71), 0),
        "norm_gain": jnp.clip(1.0 + 0.18 * jax.random.normal(streams_of[2], (D,), jnp.float32), 0.1, 1.9),
        "norm_bias": draw_norm_bias(jax.random.fold_in(streams_of[12], 71), 0),
        "decay_rate": draw_decay_rate(jax.random.fold_in(streams_of[12], 71), 0),
        "ema_angle": draw_ema_angle(jax.random.fold_in(streams_of[12], 71), 0),
        "ema_input": draw_ema_input(jax.random.fold_in(streams_of[12], 71), 0),
        "ema_output": draw_ema_output(jax.random.fold_in(streams_of[12], 71), 0),
        "ema_skip": scatter_about(streams_of[8], (D,), 0.5, 3.0, ((0, 16),), jnp.float32),
        "shared_weight": heavy_noise(streams_of[9], (D, Z), D ** -0.5, 0.125, ((0, 16),), (0, 1, 16, 2.0)),
        "shared_gain": jnp.clip(1.0 + 0.18 * jax.random.normal(streams_of[10], (Z,), jnp.float32), 0.1, 1.9),
        "output_weight": scatter_about(streams_of[11], (Z, D), Z ** -0.5, 0.1875, ((1, 16),)),
    }


precise = lax.Precision.HIGHEST
norm_eps = 1e-05
scale_eps = 1e-06

def lag_powers(decay_rate, ema_angle, count):
    lag_steps = jnp.arange(count, dtype=jnp.int32).astype(jnp.float32)[:, None, None]
    magnitude = jnp.exp(-decay_rate[None] * lag_steps)
    return (magnitude * jnp.cos(ema_angle[None] * lag_steps), magnitude * jnp.sin(ema_angle[None] * lag_steps))

def toeplitz(kernel):
    width = kernel.shape[0]
    flipped = jnp.concatenate([kernel[::-1], jnp.zeros_like(kernel)], axis=0)
    repeated = jnp.tile(flipped, (width, 1))[:width * (2 * width - 1)]
    return repeated.reshape(width, 2 * width - 1, kernel.shape[1])[:, width - 1:2 * width - 1]

def block_combine(earlier, later):
    mult_re = later[0] * earlier[0] - later[1] * earlier[1]
    mult_im = later[0] * earlier[1] + later[1] * earlier[0]
    add_re = later[0] * earlier[2] - later[1] * earlier[3] + later[2]
    add_im = later[0] * earlier[3] + later[1] * earlier[2] + later[3]
    return (mult_re, mult_im, add_re, add_im)

def group_terms(tokens):
    values = tokens.astype(jnp.float32)
    grouped = values.reshape(values.shape[0], -1, GROUP)
    return (grouped, lax.optimization_barrier(jnp.sum(grouped, axis=2)), lax.optimization_barrier(jnp.sum(grouped * grouped, axis=2)))

def timestep_norm(grouped, group_sums, group_squares, before, first_row, norm_gain, norm_bias):
    length = grouped.shape[0]
    cum_sum = before[0][None] + jnp.cumsum(group_sums, axis=0)
    cum_sq = before[1][None] + jnp.cumsum(group_squares, axis=0)
    counts = ((first_row + jnp.arange(length, dtype=jnp.int32) + 1) * GROUP).astype(jnp.float32)[:, None]
    average = cum_sum / counts
    spread = cum_sq / counts - average * average
    inverse = lax.rsqrt(spread + norm_eps)
    normed = (grouped - average[:, :, None]) * inverse[:, :, None]
    return normed.reshape(length, -1) * norm_gain[None] + norm_bias[None]

def ema_local(normed, retain, decay_rate, ema_angle, ema_input, ema_output):
    length, channels = normed.shape
    blocks = length // BLOCK
    power_real, power_im = lag_powers(decay_rate, ema_angle, BLOCK + 1)
    weight = (1.0 - jnp.exp(-decay_rate)) * ema_input
    kernel = lax.optimization_barrier(jnp.sum(weight[None] * (ema_output[0][None] * power_real[:BLOCK] - ema_output[1][None] * power_im[:BLOCK]), axis=1))
    matrix = toeplitz(kernel)
    retained = jnp.cumprod(retain.reshape(blocks, BLOCK), axis=1)
    scaled = normed.reshape(blocks, BLOCK, channels) / retained[:, :, None]
    within = jnp.einsum('tsd,bsd->btd', matrix, scaled, precision=precise)
    back_re = power_real[:BLOCK][::-1]
    back_im = power_im[:BLOCK][::-1]
    end_re = weight[None] * jnp.einsum('bsd,sjd->bjd', scaled, back_re, precision=precise)
    end_im = weight[None] * jnp.einsum('bsd,sjd->bjd', scaled, back_im, precision=precise)
    closing = retained[:, -1][:, None, None]
    elements = (closing * power_real[BLOCK][None], closing * power_im[BLOCK][None], closing * end_re, closing * end_im)
    return (within, retained, elements, (power_real, power_im))

def ema_finish(within, retained, prior_re, prior_im, powers, ema_output, normed, ema_skip):
    power_real, power_im = powers
    multiplier_cosine_part = ema_output[0][None] * power_real[1:] - ema_output[1][None] * power_im[1:]
    coeff_im = ema_output[0][None] * power_im[1:] + ema_output[1][None] * power_real[1:]
    carried_part = jnp.einsum('bjd,tjd->btd', prior_re, multiplier_cosine_part, precision=precise) - jnp.einsum('bjd,tjd->btd', prior_im, coeff_im, precision=precise)
    mixed = retained[:, :, None] * (within + carried_part)
    return mixed.reshape(normed.shape) + ema_skip[None] * normed

def reference(tokens, retain, norm_gain, norm_bias, decay_rate, ema_angle, ema_input, ema_output, ema_skip, shared_weight, shared_gain, output_weight):
    width = D // N_TENSOR
    shards = (tokens.reshape(STREAM_LENGTH, N_TENSOR, width).transpose(1, 0, 2), norm_gain.reshape(N_TENSOR, width), norm_bias.reshape(N_TENSOR, width), decay_rate.reshape(NDIM, N_TENSOR, width).transpose(1, 0, 2), ema_angle.reshape(NDIM, N_TENSOR, width).transpose(1, 0, 2), ema_input.reshape(NDIM, N_TENSOR, width).transpose(1, 0, 2), ema_output.reshape(2, NDIM, N_TENSOR, width).transpose(2, 0, 1, 3), ema_skip.reshape(N_TENSOR, width), shared_weight.reshape(N_TENSOR, width, Z))

    def add_shard(running, shard):
        tokens_part, gain_part, bias_part, rate_part, angle_part, input_part, output_part, skip_part, weight_part = shard
        grouped, group_sums, group_squares = group_terms(tokens_part)
        before = jnp.zeros((2, group_sums.shape[1]), jnp.float32)
        normed = timestep_norm(grouped, group_sums, group_squares, before, jnp.zeros((), jnp.int32), gain_part, bias_part)
        within, retained, elements, powers = ema_local(normed, retain, rate_part, angle_part, input_part, output_part)
        inclusive = lax.associative_scan(block_combine, elements)
        prior_re = jnp.concatenate([jnp.zeros_like(inclusive[2][:1]), inclusive[2][:-1]], axis=0)
        prior_im = jnp.concatenate([jnp.zeros_like(inclusive[3][:1]), inclusive[3][:-1]], axis=0)
        ema = ema_finish(within, retained, prior_re, prior_im, powers, output_part, normed, skip_part)
        active = jax.nn.silu(ema).astype(jnp.bfloat16)
        term = jnp.dot(active, weight_part, preferred_element_type=jnp.float32).astype(jnp.bfloat16)
        term = lax.optimization_barrier(term).astype(jnp.float32)
        return (running + term, None)
    shared, unused = lax.scan(add_shard, jnp.zeros((STREAM_LENGTH, Z), jnp.float32), shards)
    squares = lax.optimization_barrier(jnp.mean(shared * shared, axis=1, keepdims=True))
    common_rescaled = (shared * lax.rsqrt(squares + scale_eps) * shared_gain[None]).astype(jnp.bfloat16)
    return jnp.dot(common_rescaled, output_weight, preferred_element_type=jnp.float32).astype(jnp.bfloat16)
```

```python
import functools

import jax
import jax.numpy as jnp
from jax import lax
from jax.experimental import pallas as pl
from jax.experimental.pallas import tpu as pltpu
from jax.sharding import PartitionSpec as P

GROUP = 64
SPANS = 16
LENGTH = 256
WIDTH = 256
NDIM = 16
BLOCKS = 8
STEPS = 32
HALF = 128
CHUNK = 8

norm_eps = 1e-05
scale_eps = 1e-06

f32 = jnp.float32
bf16 = jnp.bfloat16
VMEM = pl.BlockSpec(memory_space=pltpu.VMEM)


def dot(a, b):
    return lax.dot_general(a, b, (((1,), (0,)), ((), ())), preferred_element_type=f32)


def iota2(shape, axis):
    return lax.broadcasted_iota(jnp.int32, shape, axis)


def time_of(row):
    return (row % BLOCKS) * STEPS + row // BLOCKS


def as_bf16(mask):
    return jnp.where(mask, 1.0, 0.0).astype(bf16)


def dot_parts(a, b):
    high = a.astype(bf16)
    rest = a - high.astype(f32)
    middle = rest.astype(bf16)
    low = (rest - middle.astype(f32)).astype(bf16)
    return dot(high, b) + dot(middle, b) + dot(low, b)


def cmul(ar, ai, br, bi):
    return ar * br - ai * bi, ar * bi + ai * br


def stats_kernel(tokens_ref, retain_ref, out_ref):
    values = tokens_ref[...].astype(f32)
    total = jnp.sum(values, axis=0, keepdims=True)
    squares = jnp.sum(values * values, axis=0, keepdims=True)
    kept = retain_ref[...]
    size = LENGTH
    while size > 1:
        size //= 2
        kept = kept[:, :size] * kept[:, size:]
    row = iota2((8, WIDTH), 0)
    block = jnp.where(row == 0, total, jnp.where(row == 1, squares, kept))
    for i in range(SPANS):
        out_ref[8 * i : 8 * i + 8, :] = block


def local_kernel(
    tokens_ref,
    stats_ref,
    retain_ref,
    gain_ref,
    bias_ref,
    decay_ref,
    angle_ref,
    input_ref,
    output_ref,
    message_ref,
    scaled_ref,
    retained_ref,
    state_ref,
    pack_ref,
    summary,
):
    me = lax.axis_index("span")
    before = jnp.zeros((8, WIDTH), f32)
    for i in range(SPANS):
        before += jnp.where(i < me, stats_ref[8 * i : 8 * i + 8, :], 0.0)

    tokens = tokens_ref[...]
    row = time_of(iota2((LENGTH, LENGTH), 0))
    column = iota2((LENGTH, LENGTH), 1)
    upto = as_bf16(column <= row)
    groups = as_bf16(iota2((WIDTH, WIDTH), 0) // GROUP == iota2((WIDTH, WIDTH), 1) // GROUP)
    values = tokens.astype(f32)
    squares = values * values
    high = squares.astype(bf16)
    low = (squares - high.astype(f32)).astype(bf16)
    cum_sum = dot_parts(dot(upto, tokens) + before[0:1], groups)
    cum_sq = dot_parts(dot(upto, high) + dot(upto, low) + before[1:2], groups)
    placed = dot(as_bf16(column == row), tokens)
    position = time_of(iota2((LENGTH, WIDTH), 0)) + me * LENGTH + 1
    share = 1.0 / (position * GROUP).astype(f32)
    average = cum_sum * share
    spread = cum_sq * share - average * average
    inverse = lax.rsqrt(spread + norm_eps)
    normed = (placed - average) * inverse * gain_ref[...] + bias_ref[...]

    factor = jnp.sum(jnp.where(column == row, retain_ref[...], 0.0), axis=1, keepdims=True)
    running = jnp.ones((BLOCKS, HALF), f32)
    for step in range(STEPS):
        rows = slice(BLOCKS * step, BLOCKS * step + BLOCKS)
        running = running * factor[rows]
        retained_ref[rows, :] = running
        back = 1.0 / running
        for h in range(2):
            lanes = slice(HALF * h, HALF * h + HALF)
            scaled_ref[rows, lanes] = normed[rows, lanes] * back

    decay = decay_ref[...]
    size = jnp.exp(-decay)
    power_re = size * jnp.cos(angle_ref[...])
    power_im = size * jnp.sin(angle_ref[...])
    weight = (1.0 - size) * input_ref[...]
    pack_ref[0:16, :] = power_re
    pack_ref[16:32, :] = power_im
    pack_ref[32:48, :] = output_ref[0] * weight
    pack_ref[48:64, :] = output_ref[1] * weight
    at_re, at_im = power_re, power_im
    for k in range(1, 9):
        at_re, at_im = cmul(at_re, at_im, at_re, at_im)
        if k >= 5:
            place = 64 + 32 * (k - 5)
            pack_ref[place : place + 16, :] = at_re
            pack_ref[place + 16 : place + 32, :] = at_im

    block = iota2((BLOCKS, HALF), 0)
    spans = [running]
    for k in range(2):
        reach = spans[-1]
        shifted = jnp.where(block >= 2**k, pltpu.roll(reach, 2**k, 0), 1.0)
        spans.append(reach * shifted)
    spans = [jnp.where(block >= 2**k, spans[k], 0.0) for k in range(3)]

    def wide(place, lanes):
        return jnp.broadcast_to(pack_ref[place : place + 1, lanes], (BLOCKS, HALF))

    for h in range(2):
        lanes = slice(HALF * h, HALF * h + HALF)
        for first in range(0, NDIM, CHUNK):
            js = range(first, first + CHUNK)
            re_of = [wide(j, lanes) for j in js]
            im_of = [wide(16 + j, lanes) for j in js]

            def step_on(step, held):
                u = scaled_ref[pl.ds(pl.multiple_of(step * BLOCKS, BLOCKS), BLOCKS), lanes]
                following = []
                for n in range(CHUNK):
                    re, im = held[2 * n], held[2 * n + 1]
                    following.append(re * re_of[n] - im * im_of[n] + u)
                    following.append(re * im_of[n] + im * re_of[n])
                return tuple(following)

            u0 = scaled_ref[0:BLOCKS, lanes]
            u1 = scaled_ref[BLOCKS : 2 * BLOCKS, lanes]
            begin = []
            for n in range(CHUNK):
                begin += [u0 * re_of[n] + u1, u0 * im_of[n]]
            ends = lax.fori_loop(2, STEPS, step_on, tuple(begin), unroll=3)
            for n, j in enumerate(js):
                re, im = running * ends[2 * n], running * ends[2 * n + 1]
                for k in range(3):
                    add_re, add_im = cmul(
                        pltpu.roll(re, 2**k, 0),
                        pltpu.roll(im, 2**k, 0),
                        wide(64 + 32 * k + j, lanes),
                        wide(80 + 32 * k + j, lanes),
                    )
                    re, im = re + spans[k] * add_re, im + spans[k] * add_im
                summary[j : j + 1, lanes] = re[7:8]
                summary[16 + j : 17 + j, lanes] = im[7:8]
                place = (h * NDIM + j) * 16
                state_ref[place : place + 8, :] = jnp.where(block >= 1, pltpu.roll(re, 1, 0), 0.0)
                state_ref[place + 8 : place + 16, :] = jnp.where(
                    block >= 1, pltpu.roll(im, 1, 0), 0.0
                )
    sent = summary[...].astype(bf16)
    for i in range(SPANS):
        message_ref[32 * i : 32 * i + 32, :] = sent


def finish_kernel(
    message_ref,
    stats_ref,
    scaled_ref,
    retained_ref,
    state_ref,
    pack_ref,
    skip_ref,
    weight_ref,
    give_ref,
    keep_ref,
    entering,
    mixed,
):
    me = lax.axis_index("span")
    core = lax.axis_index("tensor") % 2
    far_re, far_im = pack_ref[160:176, :], pack_ref[176:192, :]

    def turn(i, held):
        kept = stats_ref[pl.ds(i * 8 + 2, 1), :]
        piece = message_ref[pl.ds(pl.multiple_of(i * 32, 32), 32), :].astype(f32)
        re, im = cmul(held[0], held[1], far_re, far_im)
        return re * kept + piece[:16], im * kept + piece[16:]

    start = jnp.zeros((NDIM, WIDTH), f32)
    state_re, state_im = lax.fori_loop(0, me, turn, (start, start))
    entering[0:16, :] = state_re
    entering[16:32, :] = state_im

    block = iota2((BLOCKS, HALF), 0)
    closing = retained_ref[LENGTH - BLOCKS : LENGTH, :]
    ahead = jnp.where(block >= 1, pltpu.roll(closing, 1, 0), 1.0)
    for k in range(3):
        ahead = ahead * jnp.where(block >= 2**k, pltpu.roll(ahead, 2**k, 0), 1.0)

    def wide(ref, place, lanes):
        return jnp.broadcast_to(ref[place : place + 1, lanes], (BLOCKS, HALF))

    for h in range(2):
        lanes = slice(HALF * h, HALF * h + HALF)
        for first in range(0, NDIM, CHUNK):
            js = range(first, first + CHUNK)
            begin = []
            for j in js:
                re = ahead * wide(entering, j, lanes)
                im = ahead * wide(entering, 16 + j, lanes)
                for k in range(3):
                    on_re, on_im = cmul(
                        re,
                        im,
                        wide(pack_ref, 64 + 32 * k + j, lanes),
                        wide(pack_ref, 80 + 32 * k + j, lanes),
                    )
                    chosen = (block // 2**k) % 2 == 1
                    re, im = jnp.where(chosen, on_re, re), jnp.where(chosen, on_im, im)
                place = (h * NDIM + j) * 16
                begin.append(re + state_ref[place : place + 8, :])
                begin.append(im + state_ref[place + 8 : place + 16, :])
            re_of = [wide(pack_ref, j, lanes) for j in js]
            im_of = [wide(pack_ref, 16 + j, lanes) for j in js]
            out_re = [wide(pack_ref, 32 + j, lanes) for j in js]
            out_im = [wide(pack_ref, 48 + j, lanes) for j in js]
            skip = jnp.broadcast_to(skip_ref[:, lanes], (BLOCKS, HALF))

            def step_on(step, held):
                rows = pl.ds(pl.multiple_of(step * BLOCKS, BLOCKS), BLOCKS)
                u = scaled_ref[rows, lanes]
                following = []
                terms = []
                for n in range(CHUNK):
                    re, im = held[2 * n], held[2 * n + 1]
                    next_re = re * re_of[n] - im * im_of[n] + u
                    next_im = re * im_of[n] + im * re_of[n]
                    following += [next_re, next_im]
                    terms.append(out_re[n] * next_re - out_im[n] * next_im)
                while len(terms) > 1:
                    terms = [terms[i] + terms[i + 1] for i in range(0, len(terms), 2)]
                if first == 0:
                    mixed[rows, lanes] = terms[0] + skip * u
                else:
                    mixed[rows, lanes] += terms[0]
                return tuple(following)

            lax.fori_loop(0, STEPS, step_on, tuple(begin), unroll=2)

    retained = retained_ref[...]
    ema = jnp.concatenate([retained, retained], axis=1) * mixed[...]
    active = (ema / (1.0 + jnp.exp(-ema))).astype(bf16)
    slot = iota2((LENGTH, LENGTH), 0)
    side = jnp.where(slot < HALF, 1 - core, core)
    within = slot % HALF
    wanted = (within // 16) * 32 + side * 16 + within % 16
    chosen = as_bf16(time_of(iota2((LENGTH, LENGTH), 1)) == wanted)
    ordered = dot(chosen, active).astype(bf16)
    product = dot(ordered, weight_ref[...]).astype(bf16)
    give_ref[...] = product[:HALF]
    keep_ref[...] = product[HALF:]


def norm_kernel(parts_ref, gain_ref, out_ref):
    total = parts_ref[0:16, :].astype(f32)
    for i in range(1, 8):
        total += parts_ref[16 * i : 16 * i + 16, :].astype(f32)
    squares = jnp.mean(total * total, axis=1, keepdims=True)
    out_ref[...] = (total * lax.rsqrt(squares + scale_eps) * gain_ref[...]).astype(bf16)


def call(kernel, count, shapes, scratch=()):
    single = len(shapes) == 1
    made = [jax.ShapeDtypeStruct(s, d) for s, d in shapes]
    return pl.pallas_call(
        kernel,
        out_shape=made[0] if single else made,
        in_specs=[VMEM] * count,
        out_specs=VMEM if single else [VMEM] * len(shapes),
        scratch_shapes=list(scratch),
        compiler_params=pltpu.CompilerParams(vmem_limit_bytes=32 * 2**20),
    )


def shards(
    tokens,
    retain,
    norm_gain,
    norm_bias,
    decay_rate,
    ema_angle,
    ema_input,
    ema_output,
    ema_skip,
    shared_weight,
    shared_gain,
    output_weight,
):
    retain = retain.reshape(1, LENGTH)
    with jax.named_scope("stats"):
        own = call(stats_kernel, 2, [((8 * SPANS, WIDTH), f32)])(tokens, retain)
        stats = lax.all_to_all(own, "span", 0, 0, tiled=True)
    with jax.named_scope("local"):
        message, scaled, retained, state, pack = call(
            local_kernel,
            9,
            [
                ((32 * SPANS, WIDTH), bf16),
                ((LENGTH, WIDTH), f32),
                ((LENGTH, HALF), f32),
                ((2 * NDIM * 16, HALF), f32),
                ((192, WIDTH), f32),
            ],
            [pltpu.VMEM((32, WIDTH), f32)],
        )(
            tokens,
            stats,
            retain,
            norm_gain.reshape(1, WIDTH),
            norm_bias.reshape(1, WIDTH),
            decay_rate,
            ema_angle,
            ema_input,
            ema_output,
        )
        message = lax.all_to_all(message, "span", 0, 0, tiled=True)
    with jax.named_scope("finish"):
        width = shared_weight.shape[1]
        give, keep = call(
            finish_kernel,
            8,
            [((HALF, width), bf16), ((HALF, width), bf16)],
            [pltpu.VMEM((32, WIDTH), f32), pltpu.VMEM((LENGTH, WIDTH), f32)],
        )(
            message,
            stats,
            scaled,
            retained,
            state,
            pack,
            ema_skip.reshape(1, WIDTH),
            shared_weight,
        )
    with jax.named_scope("shared"):
        taken = lax.ppermute(give, "tensor", [(i, i ^ 1) for i in range(16)])
        pair = (taken.astype(f32) + keep.astype(f32)).astype(bf16)
        groups = [[core + 2 * z for z in range(8)] for core in range(2)]
        parts = lax.all_to_all(pair, "tensor", 0, 0, tiled=True, axis_index_groups=groups)
        normed = call(norm_kernel, 2, [((16, width), bf16)])(parts, shared_gain.reshape(1, width))
    with jax.named_scope("output"):
        whole = lax.all_gather(normed, "tensor", axis=0, tiled=True)
        return lax.dot_general(
            whole, output_weight, (((1,), (0,)), ((), ())), preferred_element_type=f32
        ).astype(bf16)


def solution(mesh):
    in_specs = (
        P("span", "tensor"),
        P("span"),
        P("tensor"),
        P("tensor"),
        P(None, "tensor"),
        P(None, "tensor"),
        P(None, "tensor"),
        P(None, None, "tensor"),
        P("tensor"),
        P("tensor", None),
        P(),
        P(None, "tensor"),
    )
    out_specs = P("span", "tensor")
    return jax.shard_map(shards, mesh=mesh, in_specs=in_specs, out_specs=out_specs, check_vma=False)
```

```python
import functools

import jax
import jax.numpy as jnp
from jax import lax
from jax.experimental import pallas as pl
from jax.experimental.pallas import tpu as pltpu
from jax.sharding import PartitionSpec as P

GROUP = 64
SPANS = 16
LENGTH = 256
WIDTH = 256
NDIM = 16
BLOCKS = 8
STEPS = 32
HALF = 128
CHUNK = 8

norm_eps = 1e-05
scale_eps = 1e-06

f32 = jnp.float32
bf16 = jnp.bfloat16
VMEM = pl.BlockSpec(memory_space=pltpu.VMEM)


def dot(a, b):
    return lax.dot_general(a, b, (((1,), (0,)), ((), ())), preferred_element_type=f32)


def iota2(shape, axis):
    return lax.broadcasted_iota(jnp.int32, shape, axis)


def time_of(row):
    return (row % BLOCKS) * STEPS + row // BLOCKS


def as_bf16(mask):
    return jnp.where(mask, 1.0, 0.0).astype(bf16)


def dot_parts(a, b):
    high = a.astype(bf16)
    rest = a - high.astype(f32)
    middle = rest.astype(bf16)
    low = (rest - middle.astype(f32)).astype(bf16)
    return dot(high, b) + dot(middle, b) + dot(low, b)


def cmul(ar, ai, br, bi):
    return ar * br - ai * bi, ar * bi + ai * br


def stats_kernel(tokens_hbm, retain_hbm, out_ref, tokens_ref, retain_ref, arrived):
    copies = (
        pltpu.make_async_copy(tokens_hbm, tokens_ref, arrived.at[0]),
        pltpu.make_async_copy(retain_hbm, retain_ref, arrived.at[1]),
    )
    for copy in copies:
        copy.start()
    for copy in copies:
        copy.wait()
    values = tokens_ref[...].astype(f32)
    total = jnp.sum(values, axis=0, keepdims=True)
    squares = jnp.sum(values * values, axis=0, keepdims=True)
    kept = retain_ref[...]
    size = LENGTH
    while size > 1:
        size //= 2
        kept = kept[:, :size] * kept[:, size:]
    row = iota2((8, WIDTH), 0)
    block = jnp.where(row == 0, total, jnp.where(row == 1, squares, kept))
    for i in range(SPANS):
        out_ref[8 * i : 8 * i + 8, :] = block


def local_kernel(
    tokens_ref,
    stats_ref,
    retain_ref,
    gain_ref,
    bias_ref,
    decay_ref,
    angle_ref,
    input_ref,
    output_ref,
    skip_ref,
    message_ref,
    scaled_ref,
    retained_ref,
    state_ref,
    pack_ref,
    summary,
):
    me = lax.axis_index("span")
    before = jnp.zeros((8, WIDTH), f32)
    for i in range(SPANS):
        before += jnp.where(i < me, stats_ref[8 * i : 8 * i + 8, :], 0.0)

    tokens = tokens_ref[...]
    row = time_of(iota2((LENGTH, LENGTH), 0))
    column = iota2((LENGTH, LENGTH), 1)
    upto = as_bf16(column <= row)
    groups = as_bf16(iota2((WIDTH, WIDTH), 0) // GROUP == iota2((WIDTH, WIDTH), 1) // GROUP)
    values = tokens.astype(f32)
    squares = values * values
    high = squares.astype(bf16)
    low = (squares - high.astype(f32)).astype(bf16)
    cum_sum = dot_parts(dot(upto, tokens) + before[0:1], groups)
    cum_sq = dot_parts(dot(upto, high) + dot(upto, low) + before[1:2], groups)
    placed = dot(as_bf16(column == row), tokens)
    position = time_of(iota2((LENGTH, WIDTH), 0)) + me * LENGTH + 1
    share = 1.0 / (position * GROUP).astype(f32)
    average = cum_sum * share
    spread = cum_sq * share - average * average
    inverse = lax.rsqrt(spread + norm_eps)
    normed = (placed - average) * inverse * gain_ref[...] + bias_ref[...]

    factor = jnp.sum(jnp.where(column == row, retain_ref[...], 0.0), axis=1, keepdims=True)
    running = jnp.ones((BLOCKS, HALF), f32)
    for step in range(STEPS):
        rows = slice(BLOCKS * step, BLOCKS * step + BLOCKS)
        running = running * factor[rows]
        retained_ref[rows, :] = running
        back = 1.0 / running
        for h in range(2):
            lanes = slice(HALF * h, HALF * h + HALF)
            scaled_ref[rows, lanes] = normed[rows, lanes] * back

    decay = decay_ref[...]
    size = jnp.exp(-decay)
    power_re = size * jnp.cos(angle_ref[...])
    power_im = size * jnp.sin(angle_ref[...])
    weight = (1.0 - size) * input_ref[...]
    pack_ref[0:16, :] = power_re
    pack_ref[16:32, :] = power_im
    pack_ref[32:48, :] = output_ref[0] * weight
    pack_ref[48:64, :] = output_ref[1] * weight
    pack_ref[192:200, :] = jnp.broadcast_to(skip_ref[...], (8, WIDTH))
    at_re, at_im = power_re, power_im
    for k in range(1, 9):
        at_re, at_im = cmul(at_re, at_im, at_re, at_im)
        if k >= 5:
            place = 64 + 32 * (k - 5)
            pack_ref[place : place + 16, :] = at_re
            pack_ref[place + 16 : place + 32, :] = at_im

    block = iota2((BLOCKS, HALF), 0)
    spans = [running]
    for k in range(2):
        reach = spans[-1]
        shifted = jnp.where(block >= 2**k, pltpu.roll(reach, 2**k, 0), 1.0)
        spans.append(reach * shifted)
    spans = [jnp.where(block >= 2**k, spans[k], 0.0) for k in range(3)]

    def wide(place, lanes):
        return jnp.broadcast_to(pack_ref[place : place + 1, lanes], (BLOCKS, HALF))

    for h in range(2):
        lanes = slice(HALF * h, HALF * h + HALF)
        for first in range(0, NDIM, CHUNK):
            js = range(first, first + CHUNK)
            re_of = [wide(j, lanes) for j in js]
            im_of = [wide(16 + j, lanes) for j in js]

            def step_on(step, held):
                u = scaled_ref[pl.ds(pl.multiple_of(step * BLOCKS, BLOCKS), BLOCKS), lanes]
                following = []
                for n in range(CHUNK):
                    re, im = held[2 * n], held[2 * n + 1]
                    following.append(re * re_of[n] - im * im_of[n] + u)
                    following.append(re * im_of[n] + im * re_of[n])
                return tuple(following)

            u0 = scaled_ref[0:BLOCKS, lanes]
            u1 = scaled_ref[BLOCKS : 2 * BLOCKS, lanes]
            begin = []
            for n in range(CHUNK):
                begin += [u0 * re_of[n] + u1, u0 * im_of[n]]
            ends = lax.fori_loop(2, STEPS, step_on, tuple(begin), unroll=3)
            for n, j in enumerate(js):
                re, im = running * ends[2 * n], running * ends[2 * n + 1]
                for k in range(3):
                    add_re, add_im = cmul(
                        pltpu.roll(re, 2**k, 0),
                        pltpu.roll(im, 2**k, 0),
                        wide(64 + 32 * k + j, lanes),
                        wide(80 + 32 * k + j, lanes),
                    )
                    re, im = re + spans[k] * add_re, im + spans[k] * add_im
                summary[j : j + 1, lanes] = re[7:8]
                summary[16 + j : 17 + j, lanes] = im[7:8]
                place = (h * NDIM + j) * 16
                state_ref[place : place + 8, :] = jnp.where(block >= 1, pltpu.roll(re, 1, 0), 0.0)
                state_ref[place + 8 : place + 16, :] = jnp.where(
                    block >= 1, pltpu.roll(im, 1, 0), 0.0
                )
    sent = summary[...].astype(bf16)
    for i in range(SPANS):
        message_ref[32 * i : 32 * i + 32, :] = sent


def finish_kernel(
    message_ref,
    stats_ref,
    scaled_ref,
    retained_ref,
    state_ref,
    pack_ref,
    weight_ref,
    give_ref,
    keep_ref,
    entering,
    mixed,
):
    me = lax.axis_index("span")
    core = lax.axis_index("tensor") % 2
    far_re, far_im = pack_ref[160:176, :], pack_ref[176:192, :]

    def turn(i, held):
        kept = stats_ref[pl.ds(i * 8 + 2, 1), :]
        piece = message_ref[pl.ds(pl.multiple_of(i * 32, 32), 32), :].astype(f32)
        re, im = cmul(held[0], held[1], far_re, far_im)
        return re * kept + piece[:16], im * kept + piece[16:]

    start = jnp.zeros((NDIM, WIDTH), f32)
    state_re, state_im = lax.fori_loop(0, me, turn, (start, start))
    entering[0:16, :] = state_re
    entering[16:32, :] = state_im

    block = iota2((BLOCKS, HALF), 0)
    closing = retained_ref[LENGTH - BLOCKS : LENGTH, :]
    ahead = jnp.where(block >= 1, pltpu.roll(closing, 1, 0), 1.0)
    for k in range(3):
        ahead = ahead * jnp.where(block >= 2**k, pltpu.roll(ahead, 2**k, 0), 1.0)

    def wide(ref, place, lanes):
        return jnp.broadcast_to(ref[place : place + 1, lanes], (BLOCKS, HALF))

    for h in range(2):
        lanes = slice(HALF * h, HALF * h + HALF)
        for first in range(0, NDIM, CHUNK):
            js = range(first, first + CHUNK)
            begin = []
            for j in js:
                re = ahead * wide(entering, j, lanes)
                im = ahead * wide(entering, 16 + j, lanes)
                for k in range(3):
                    on_re, on_im = cmul(
                        re,
                        im,
                        wide(pack_ref, 64 + 32 * k + j, lanes),
                        wide(pack_ref, 80 + 32 * k + j, lanes),
                    )
                    chosen = (block // 2**k) % 2 == 1
                    re, im = jnp.where(chosen, on_re, re), jnp.where(chosen, on_im, im)
                place = (h * NDIM + j) * 16
                begin.append(re + state_ref[place : place + 8, :])
                begin.append(im + state_ref[place + 8 : place + 16, :])
            re_of = [wide(pack_ref, j, lanes) for j in js]
            im_of = [wide(pack_ref, 16 + j, lanes) for j in js]
            out_re = [wide(pack_ref, 32 + j, lanes) for j in js]
            out_im = [wide(pack_ref, 48 + j, lanes) for j in js]
            skip = pack_ref[192:200, lanes]

            def step_on(step, held):
                rows = pl.ds(pl.multiple_of(step * BLOCKS, BLOCKS), BLOCKS)
                u = scaled_ref[rows, lanes]
                following = []
                terms = []
                for n in range(CHUNK):
                    re, im = held[2 * n], held[2 * n + 1]
                    next_re = re * re_of[n] - im * im_of[n] + u
                    next_im = re * im_of[n] + im * re_of[n]
                    following += [next_re, next_im]
                    terms.append(out_re[n] * next_re - out_im[n] * next_im)
                while len(terms) > 1:
                    terms = [terms[i] + terms[i + 1] for i in range(0, len(terms), 2)]
                if first == 0:
                    mixed[rows, lanes] = terms[0] + skip * u
                else:
                    mixed[rows, lanes] += terms[0]
                return tuple(following)

            lax.fori_loop(0, STEPS, step_on, tuple(begin), unroll=2)

    retained = retained_ref[...]
    ema = jnp.concatenate([retained, retained], axis=1) * mixed[...]
    active = (ema / (1.0 + jnp.exp(-ema))).astype(bf16)
    slot = iota2((LENGTH, LENGTH), 0)
    wanted = (slot + (1 - core) * HALF) % LENGTH
    chosen = as_bf16(time_of(iota2((LENGTH, LENGTH), 1)) == wanted)
    ordered = dot(chosen, active).astype(bf16)
    product = dot(ordered, weight_ref[...]).astype(bf16)
    give_ref[...] = product[:HALF]
    keep_ref[...] = product[HALF:]


def norm_kernel(parts_ref, gain_ref, out_ref):
    total = parts_ref[0:16, :].astype(f32)
    for i in range(1, 8):
        total += parts_ref[16 * i : 16 * i + 16, :].astype(f32)
    squares = jnp.mean(total * total, axis=1, keepdims=True)
    normed = (total * lax.rsqrt(squares + scale_eps) * gain_ref[...]).astype(bf16)
    for i in range(8):
        out_ref[16 * i : 16 * i + 16, :] = normed


def output_kernel(shared_ref, weight_ref, out_ref):
    out_ref[...] = dot(shared_ref[...], weight_ref[...]).astype(bf16)


def call(kernel, count, shapes, scratch=(), space=VMEM, limit=32):
    single = len(shapes) == 1
    made = [jax.ShapeDtypeStruct(s, d) for s, d in shapes]
    return pl.pallas_call(
        kernel,
        out_shape=made[0] if single else made,
        in_specs=[space] * count,
        out_specs=VMEM if single else [VMEM] * len(shapes),
        scratch_shapes=list(scratch),
        compiler_params=pltpu.CompilerParams(vmem_limit_bytes=limit * 2**20),
    )


def shards(
    tokens,
    retain,
    norm_gain,
    norm_bias,
    decay_rate,
    ema_angle,
    ema_input,
    ema_output,
    ema_skip,
    shared_weight,
    shared_gain,
    output_weight,
):
    retain = retain.reshape(1, LENGTH)
    with jax.named_scope("stats"):
        own = call(
            stats_kernel,
            2,
            [((8 * SPANS, WIDTH), f32)],
            [
                pltpu.VMEM((LENGTH, WIDTH), bf16),
                pltpu.VMEM((1, LENGTH), f32),
                pltpu.SemaphoreType.DMA((2,)),
            ],
            pl.BlockSpec(memory_space=pltpu.HBM),
            60,
        )(tokens, retain)
        stats = lax.all_to_all(own, "span", 0, 0, tiled=True)
    with jax.named_scope("local"):
        message, scaled, retained, state, pack = call(
            local_kernel,
            10,
            [
                ((32 * SPANS, WIDTH), bf16),
                ((LENGTH, WIDTH), f32),
                ((LENGTH, HALF), f32),
                ((2 * NDIM * 16, HALF), f32),
                ((200, WIDTH), f32),
            ],
            [pltpu.VMEM((32, WIDTH), f32)],
        )(
            tokens,
            stats,
            retain,
            norm_gain.reshape(1, WIDTH),
            norm_bias.reshape(1, WIDTH),
            decay_rate,
            ema_angle,
            ema_input,
            ema_output,
            ema_skip.reshape(1, WIDTH),
        )
        message = lax.all_to_all(message, "span", 0, 0, tiled=True)
    with jax.named_scope("finish"):
        width = shared_weight.shape[1]
        give, keep = call(
            finish_kernel,
            7,
            [((HALF, width), bf16), ((HALF, width), bf16)],
            [pltpu.VMEM((32, WIDTH), f32), pltpu.VMEM((LENGTH, WIDTH), f32)],
        )(
            message,
            stats,
            scaled,
            retained,
            state,
            pack,
            shared_weight,
        )
    with jax.named_scope("shared"):
        taken = lax.ppermute(give, "tensor", [(i, i ^ 1) for i in range(16)])
        pair = (taken.astype(f32) + keep.astype(f32)).astype(bf16)
        groups = [[core + 2 * z for z in range(8)] for core in range(2)]
        parts = lax.all_to_all(pair, "tensor", 0, 0, tiled=True, axis_index_groups=groups)
        copies = call(norm_kernel, 2, [((HALF, width), bf16)])(parts, shared_gain.reshape(1, width))
    with jax.named_scope("output"):
        half = lax.all_to_all(copies, "tensor", 0, 0, tiled=True, axis_index_groups=groups)
        pairs = [[2 * z, 2 * z + 1] for z in range(8)]
        whole = lax.all_gather(half, "tensor", axis=0, tiled=True, axis_index_groups=pairs)
        return call(output_kernel, 2, [((LENGTH, WIDTH), bf16)])(whole, output_weight)


def solution(mesh):
    in_specs = (
        P("span", "tensor"),
        P("span"),
        P("tensor"),
        P("tensor"),
        P(None, "tensor"),
        P(None, "tensor"),
        P(None, "tensor"),
        P(None, None, "tensor"),
        P("tensor"),
        P("tensor", None),
        P(),
        P(None, "tensor"),
    )
    out_specs = P("span", "tensor")
    return jax.shard_map(shards, mesh=mesh, in_specs=in_specs, out_specs=out_specs, check_vma=False)
```

```python
import functools

import jax
import jax.numpy as jnp
from jax import lax
from jax.experimental import pallas as pl
from jax.experimental.pallas import tpu as pltpu
from jax.sharding import PartitionSpec as P

GROUP = 64
SPANS = 16
LENGTH = 256
WIDTH = 256
NDIM = 16
BLOCKS = 8
STEPS = 32
HALF = 128
CHUNK = 8

norm_eps = 1e-05
scale_eps = 1e-06

f32 = jnp.float32
bf16 = jnp.bfloat16
VMEM = pl.BlockSpec(memory_space=pltpu.VMEM)


def dot(a, b):
    return lax.dot_general(a, b, (((1,), (0,)), ((), ())), preferred_element_type=f32)


def iota2(shape, axis):
    return lax.broadcasted_iota(jnp.int32, shape, axis)


def time_of(row):
    return (row % BLOCKS) * STEPS + row // BLOCKS


def as_bf16(mask):
    return jnp.where(mask, 1.0, 0.0).astype(bf16)


def dot_parts(a, b):
    high = a.astype(bf16)
    rest = a - high.astype(f32)
    middle = rest.astype(bf16)
    low = (rest - middle.astype(f32)).astype(bf16)
    return dot(high, b) + dot(middle, b) + dot(low, b)


def cmul(ar, ai, br, bi):
    return ar * br - ai * bi, ar * bi + ai * br


def stats_kernel(tokens_hbm, retain_hbm, out_ref, tokens_ref, retain_ref, arrived):
    copies = (
        pltpu.make_async_copy(tokens_hbm, tokens_ref, arrived.at[0]),
        pltpu.make_async_copy(retain_hbm, retain_ref, arrived.at[1]),
    )
    for copy in copies:
        copy.start()
    for copy in copies:
        copy.wait()
    values = tokens_ref[...].astype(f32)
    total = jnp.sum(values, axis=0, keepdims=True)
    squares = jnp.sum(values * values, axis=0, keepdims=True)
    kept = retain_ref[...]
    size = LENGTH
    while size > 1:
        size //= 2
        kept = kept[:, :size] * kept[:, size:]
    row = iota2((8, WIDTH), 0)
    block = jnp.where(row == 0, total, jnp.where(row == 1, squares, kept))
    for i in range(SPANS):
        out_ref[8 * i : 8 * i + 8, :] = block


def prepare_kernel(
    tokens_ref,
    retain_ref,
    decay_ref,
    angle_ref,
    input_ref,
    output_ref,
    skip_ref,
    sums_ref,
    squares_ref,
    placed_ref,
    retained_ref,
    back_ref,
    pack_ref,
):
    tokens = tokens_ref[...]
    row = time_of(iota2((LENGTH, LENGTH), 0))
    column = iota2((LENGTH, LENGTH), 1)
    upto = as_bf16(column <= row)
    values = tokens.astype(f32)
    squares = values * values
    high = squares.astype(bf16)
    low = (squares - high.astype(f32)).astype(bf16)
    sums_ref[...] = dot(upto, tokens)
    squares_ref[...] = dot(upto, high) + dot(upto, low)
    placed_ref[...] = dot(as_bf16(column == row), tokens)

    factor = jnp.sum(jnp.where(column == row, retain_ref[...], 0.0), axis=1, keepdims=True)
    running = jnp.ones((BLOCKS, HALF), f32)
    for step in range(STEPS):
        rows = slice(BLOCKS * step, BLOCKS * step + BLOCKS)
        running = running * factor[rows]
        retained_ref[rows, :] = running
        back_ref[rows, :] = 1.0 / running

    decay = decay_ref[...]
    size = jnp.exp(-decay)
    power_re = size * jnp.cos(angle_ref[...])
    power_im = size * jnp.sin(angle_ref[...])
    weight = (1.0 - size) * input_ref[...]
    pack_ref[0:16, :] = power_re
    pack_ref[16:32, :] = power_im
    pack_ref[32:48, :] = output_ref[0] * weight
    pack_ref[48:64, :] = output_ref[1] * weight
    pack_ref[192:200, :] = jnp.broadcast_to(skip_ref[...], (8, WIDTH))
    at_re, at_im = power_re, power_im
    for k in range(1, 9):
        at_re, at_im = cmul(at_re, at_im, at_re, at_im)
        if k >= 5:
            place = 64 + 32 * (k - 5)
            pack_ref[place : place + 16, :] = at_re
            pack_ref[place + 16 : place + 32, :] = at_im

def local_kernel(
    stats_ref,
    sums_ref,
    squares_ref,
    placed_ref,
    retained_ref,
    back_ref,
    pack_ref,
    gain_ref,
    bias_ref,
    message_ref,
    scaled_ref,
    state_ref,
    summary,
):
    me = lax.axis_index("span")
    before = jnp.zeros((8, WIDTH), f32)
    for i in range(SPANS):
        before += jnp.where(i < me, stats_ref[8 * i : 8 * i + 8, :], 0.0)

    groups = as_bf16(iota2((WIDTH, WIDTH), 0) // GROUP == iota2((WIDTH, WIDTH), 1) // GROUP)
    cum_sum = dot_parts(sums_ref[...] + before[0:1], groups)
    cum_sq = dot_parts(squares_ref[...] + before[1:2], groups)
    position = time_of(iota2((LENGTH, WIDTH), 0)) + me * LENGTH + 1
    share = 1.0 / (position * GROUP).astype(f32)
    average = cum_sum * share
    spread = cum_sq * share - average * average
    inverse = lax.rsqrt(spread + norm_eps)
    normed = (placed_ref[...] - average) * inverse * gain_ref[...] + bias_ref[...]
    back = back_ref[...]
    scaled_ref[...] = normed * jnp.concatenate([back, back], axis=1)
    running = retained_ref[LENGTH - BLOCKS : LENGTH, :]

    block = iota2((BLOCKS, HALF), 0)
    spans = [running]
    for k in range(2):
        reach = spans[-1]
        shifted = jnp.where(block >= 2**k, pltpu.roll(reach, 2**k, 0), 1.0)
        spans.append(reach * shifted)
    spans = [jnp.where(block >= 2**k, spans[k], 0.0) for k in range(3)]

    def wide(place, lanes):
        return jnp.broadcast_to(pack_ref[place : place + 1, lanes], (BLOCKS, HALF))

    for h in range(2):
        lanes = slice(HALF * h, HALF * h + HALF)
        for first in range(0, NDIM, CHUNK):
            js = range(first, first + CHUNK)
            re_of = [wide(j, lanes) for j in js]
            im_of = [wide(16 + j, lanes) for j in js]

            def step_on(step, held):
                u = scaled_ref[pl.ds(pl.multiple_of(step * BLOCKS, BLOCKS), BLOCKS), lanes]
                following = []
                for n in range(CHUNK):
                    re, im = held[2 * n], held[2 * n + 1]
                    following.append(re * re_of[n] - im * im_of[n] + u)
                    following.append(re * im_of[n] + im * re_of[n])
                return tuple(following)

            u0 = scaled_ref[0:BLOCKS, lanes]
            u1 = scaled_ref[BLOCKS : 2 * BLOCKS, lanes]
            begin = []
            for n in range(CHUNK):
                begin += [u0 * re_of[n] + u1, u0 * im_of[n]]
            ends = lax.fori_loop(2, STEPS, step_on, tuple(begin), unroll=3)
            for n, j in enumerate(js):
                re, im = running * ends[2 * n], running * ends[2 * n + 1]
                for k in range(3):
                    add_re, add_im = cmul(
                        pltpu.roll(re, 2**k, 0),
                        pltpu.roll(im, 2**k, 0),
                        wide(64 + 32 * k + j, lanes),
                        wide(80 + 32 * k + j, lanes),
                    )
                    re, im = re + spans[k] * add_re, im + spans[k] * add_im
                summary[j : j + 1, lanes] = re[7:8]
                summary[16 + j : 17 + j, lanes] = im[7:8]
                place = (h * NDIM + j) * 16
                state_ref[place : place + 8, :] = jnp.where(block >= 1, pltpu.roll(re, 1, 0), 0.0)
                state_ref[place + 8 : place + 16, :] = jnp.where(
                    block >= 1, pltpu.roll(im, 1, 0), 0.0
                )
    sent = summary[...].astype(bf16)
    for i in range(SPANS):
        message_ref[32 * i : 32 * i + 32, :] = sent


def finish_kernel(
    message_ref,
    stats_ref,
    scaled_ref,
    retained_ref,
    state_ref,
    pack_ref,
    weight_ref,
    give_ref,
    keep_ref,
    entering,
    mixed,
):
    me = lax.axis_index("span")
    core = lax.axis_index("tensor") % 2
    far_re, far_im = pack_ref[160:176, :], pack_ref[176:192, :]

    def turn(i, held):
        kept = stats_ref[pl.ds(i * 8 + 2, 1), :]
        piece = message_ref[pl.ds(pl.multiple_of(i * 32, 32), 32), :].astype(f32)
        re, im = cmul(held[0], held[1], far_re, far_im)
        return re * kept + piece[:16], im * kept + piece[16:]

    start = jnp.zeros((NDIM, WIDTH), f32)
    state_re, state_im = lax.fori_loop(0, me, turn, (start, start))
    entering[0:16, :] = state_re
    entering[16:32, :] = state_im

    block = iota2((BLOCKS, HALF), 0)
    closing = retained_ref[LENGTH - BLOCKS : LENGTH, :]
    ahead = jnp.where(block >= 1, pltpu.roll(closing, 1, 0), 1.0)
    for k in range(3):
        ahead = ahead * jnp.where(block >= 2**k, pltpu.roll(ahead, 2**k, 0), 1.0)

    def wide(ref, place, lanes):
        return jnp.broadcast_to(ref[place : place + 1, lanes], (BLOCKS, HALF))

    for h in range(2):
        lanes = slice(HALF * h, HALF * h + HALF)
        for first in range(0, NDIM, CHUNK):
            js = range(first, first + CHUNK)
            begin = []
            for j in js:
                re = ahead * wide(entering, j, lanes)
                im = ahead * wide(entering, 16 + j, lanes)
                for k in range(3):
                    on_re, on_im = cmul(
                        re,
                        im,
                        wide(pack_ref, 64 + 32 * k + j, lanes),
                        wide(pack_ref, 80 + 32 * k + j, lanes),
                    )
                    chosen = (block // 2**k) % 2 == 1
                    re, im = jnp.where(chosen, on_re, re), jnp.where(chosen, on_im, im)
                place = (h * NDIM + j) * 16
                begin.append(re + state_ref[place : place + 8, :])
                begin.append(im + state_ref[place + 8 : place + 16, :])
            re_of = [wide(pack_ref, j, lanes) for j in js]
            im_of = [wide(pack_ref, 16 + j, lanes) for j in js]
            out_re = [wide(pack_ref, 32 + j, lanes) for j in js]
            out_im = [wide(pack_ref, 48 + j, lanes) for j in js]
            skip = pack_ref[192:200, lanes]

            def step_on(step, held):
                rows = pl.ds(pl.multiple_of(step * BLOCKS, BLOCKS), BLOCKS)
                u = scaled_ref[rows, lanes]
                following = []
                terms = []
                for n in range(CHUNK):
                    re, im = held[2 * n], held[2 * n + 1]
                    next_re = re * re_of[n] - im * im_of[n] + u
                    next_im = re * im_of[n] + im * re_of[n]
                    following += [next_re, next_im]
                    terms.append(out_re[n] * next_re - out_im[n] * next_im)
                while len(terms) > 1:
                    terms = [terms[i] + terms[i + 1] for i in range(0, len(terms), 2)]
                if first == 0:
                    mixed[rows, lanes] = terms[0] + skip * u
                else:
                    mixed[rows, lanes] += terms[0]
                return tuple(following)

            lax.fori_loop(0, STEPS, step_on, tuple(begin), unroll=2)

    retained = retained_ref[...]
    ema = jnp.concatenate([retained, retained], axis=1) * mixed[...]
    active = (ema / (1.0 + jnp.exp(-ema))).astype(bf16)
    slot = iota2((LENGTH, LENGTH), 0)
    wanted = (slot + (1 - core) * HALF) % LENGTH
    chosen = as_bf16(time_of(iota2((LENGTH, LENGTH), 1)) == wanted)
    ordered = dot(chosen, active).astype(bf16)
    product = dot(ordered, weight_ref[...]).astype(bf16)
    give_ref[...] = product[:HALF]
    keep_ref[...] = product[HALF:]


def norm_kernel(parts_ref, gain_ref, out_ref):
    total = parts_ref[0:16, :].astype(f32)
    for i in range(1, 8):
        total += parts_ref[16 * i : 16 * i + 16, :].astype(f32)
    squares = jnp.mean(total * total, axis=1, keepdims=True)
    normed = (total * lax.rsqrt(squares + scale_eps) * gain_ref[...]).astype(bf16)
    for i in range(8):
        out_ref[16 * i : 16 * i + 16, :] = normed


def output_kernel(shared_ref, weight_ref, out_ref):
    out_ref[...] = dot(shared_ref[...], weight_ref[...]).astype(bf16)


def call(kernel, count, shapes, scratch=(), space=VMEM, limit=32, cost=None):
    single = len(shapes) == 1
    made = [jax.ShapeDtypeStruct(s, d) for s, d in shapes]
    return pl.pallas_call(
        kernel,
        out_shape=made[0] if single else made,
        in_specs=[space] * count,
        out_specs=VMEM if single else [VMEM] * len(shapes),
        scratch_shapes=list(scratch),
        compiler_params=pltpu.CompilerParams(vmem_limit_bytes=limit * 2**20),
        cost_estimate=cost,
    )


def shards(
    tokens,
    retain,
    norm_gain,
    norm_bias,
    decay_rate,
    ema_angle,
    ema_input,
    ema_output,
    ema_skip,
    shared_weight,
    shared_gain,
    output_weight,
):
    retain = retain.reshape(1, LENGTH)
    with jax.named_scope("stats"):
        own = call(
            stats_kernel,
            2,
            [((8 * SPANS, WIDTH), f32)],
            [
                pltpu.VMEM((LENGTH, WIDTH), bf16),
                pltpu.VMEM((1, LENGTH), f32),
                pltpu.SemaphoreType.DMA((2,)),
            ],
            pl.BlockSpec(memory_space=pltpu.HBM),
            60,
        )(tokens, retain)
        stats = lax.all_to_all(own, "span", 0, 0, tiled=True)
    with jax.named_scope("local"):
        sums, squares, placed, retained, back, pack = call(
            prepare_kernel,
            7,
            [((LENGTH, WIDTH), f32)] * 3 + [((LENGTH, HALF), f32)] * 2 + [((200, WIDTH), f32)],
            cost=pl.CostEstimate(flops=2 * 10**9, bytes_accessed=2**22, transcendentals=0),
        )(
            tokens,
            retain,
            decay_rate,
            ema_angle,
            ema_input,
            ema_output,
            ema_skip.reshape(1, WIDTH),
        )
        message, scaled, state = call(
            local_kernel,
            9,
            [
                ((32 * SPANS, WIDTH), bf16),
                ((LENGTH, WIDTH), f32),
                ((2 * NDIM * 16, HALF), f32),
            ],
            [pltpu.VMEM((32, WIDTH), f32)],
        )(
            stats,
            sums,
            squares,
            placed,
            retained,
            back,
            pack,
            norm_gain.reshape(1, WIDTH),
            norm_bias.reshape(1, WIDTH),
        )
        message = lax.all_to_all(message, "span", 0, 0, tiled=True)
    with jax.named_scope("finish"):
        width = shared_weight.shape[1]
        give, keep = call(
            finish_kernel,
            7,
            [((HALF, width), bf16), ((HALF, width), bf16)],
            [pltpu.VMEM((32, WIDTH), f32), pltpu.VMEM((LENGTH, WIDTH), f32)],
        )(
            message,
            stats,
            scaled,
            retained,
            state,
            pack,
            shared_weight,
        )
    with jax.named_scope("shared"):
        taken = lax.ppermute(give, "tensor", [(i, i ^ 1) for i in range(16)])
        pair = (taken.astype(f32) + keep.astype(f32)).astype(bf16)
        groups = [[core + 2 * z for z in range(8)] for core in range(2)]
        parts = lax.all_to_all(pair, "tensor", 0, 0, tiled=True, axis_index_groups=groups)
        copies = call(norm_kernel, 2, [((HALF, width), bf16)])(parts, shared_gain.reshape(1, width))
    with jax.named_scope("output"):
        half = lax.all_to_all(copies, "tensor", 0, 0, tiled=True, axis_index_groups=groups)
        pairs = [[2 * z, 2 * z + 1] for z in range(8)]
        whole = lax.all_gather(half, "tensor", axis=0, tiled=True, axis_index_groups=pairs)
        return call(output_kernel, 2, [((LENGTH, WIDTH), bf16)])(whole, output_weight)


def solution(mesh):
    in_specs = (
        P("span", "tensor"),
        P("span"),
        P("tensor"),
        P("tensor"),
        P(None, "tensor"),
        P(None, "tensor"),
        P(None, "tensor"),
        P(None, None, "tensor"),
        P("tensor"),
        P("tensor", None),
        P(),
        P(None, "tensor"),
    )
    out_specs = P("span", "tensor")
    return jax.shard_map(shards, mesh=mesh, in_specs=in_specs, out_specs=out_specs, check_vma=False)
```

```python
import functools

import jax
import jax.numpy as jnp
from jax import lax
from jax.experimental import pallas as pl
from jax.experimental.pallas import tpu as pltpu
from jax.sharding import PartitionSpec as P

GROUP = 64
SPANS = 16
LENGTH = 256
WIDTH = 256
NDIM = 16
BLOCKS = 8
STEPS = 32
HALF = 128
CHUNK = 8

norm_eps = 1e-05
scale_eps = 1e-06

f32 = jnp.float32
bf16 = jnp.bfloat16
VMEM = pl.BlockSpec(memory_space=pltpu.VMEM)


def dot(a, b):
    return lax.dot_general(a, b, (((1,), (0,)), ((), ())), preferred_element_type=f32)


def iota2(shape, axis):
    return lax.broadcasted_iota(jnp.int32, shape, axis)


def time_of(row):
    return (row % BLOCKS) * STEPS + row // BLOCKS


def as_bf16(mask):
    return jnp.where(mask, 1.0, 0.0).astype(bf16)


def dot_parts(a, b):
    high = a.astype(bf16)
    rest = a - high.astype(f32)
    middle = rest.astype(bf16)
    low = (rest - middle.astype(f32)).astype(bf16)
    return dot(high, b) + dot(middle, b) + dot(low, b)


def cmul(ar, ai, br, bi):
    return ar * br - ai * bi, ar * bi + ai * br


def stats_kernel(tokens_ref, retain_ref, out_ref):
    values = tokens_ref[...].astype(f32)
    total = jnp.sum(values, axis=0, keepdims=True)
    squares = jnp.sum(values * values, axis=0, keepdims=True)
    kept = retain_ref[...]
    size = LENGTH
    while size > 1:
        size //= 2
        kept = kept[:, :size] * kept[:, size:]
    row = iota2((8, WIDTH), 0)
    block = jnp.where(row == 0, total, jnp.where(row == 1, squares, kept))
    for i in range(SPANS):
        out_ref[8 * i : 8 * i + 8, :] = block


def prepare_kernel(
    tokens_ref,
    retain_ref,
    decay_ref,
    angle_ref,
    input_ref,
    output_ref,
    skip_ref,
    gain_ref,
    bias_ref,
    sums_ref,
    squares_ref,
    placed_ref,
    retained_ref,
    back_ref,
    pack_ref,
    leave_ref,
    enter_ref,
    power_ref,
):
    tokens = tokens_ref[...]
    row = time_of(iota2((LENGTH, LENGTH), 0))
    column = iota2((LENGTH, LENGTH), 1)
    upto = as_bf16(column <= row)
    values = tokens.astype(f32)
    squares = values * values
    high = squares.astype(bf16)
    low = (squares - high.astype(f32)).astype(bf16)
    sums_ref[...] = dot(upto, tokens)
    squares_ref[...] = dot(upto, high) + dot(upto, low)
    placed_ref[...] = dot(as_bf16(column == row), tokens)

    factor = jnp.sum(jnp.where(column == row, retain_ref[...], 0.0), axis=1, keepdims=True)
    running = jnp.ones((BLOCKS, HALF), f32)
    for step in range(STEPS):
        rows = slice(BLOCKS * step, BLOCKS * step + BLOCKS)
        running = running * factor[rows]
        retained_ref[rows, :] = running
        back_ref[rows, :] = 1.0 / running

    decay = decay_ref[...]
    size = jnp.exp(-decay)
    power_re = size * jnp.cos(angle_ref[...])
    power_im = size * jnp.sin(angle_ref[...])
    weight = (1.0 - size) * input_ref[...]
    pack_ref[0:16, :] = power_re
    pack_ref[16:32, :] = power_im
    pack_ref[32:48, :] = output_ref[0] * weight
    pack_ref[48:64, :] = output_ref[1] * weight
    pack_ref[192:200, :] = jnp.broadcast_to(skip_ref[...], (8, WIDTH))
    pack_ref[200:208, :] = jnp.broadcast_to(gain_ref[...], (8, WIDTH))
    pack_ref[208:216, :] = jnp.broadcast_to(bias_ref[...], (8, WIDTH))
    at_re, at_im = power_re, power_im
    for k in range(1, 9):
        at_re, at_im = cmul(at_re, at_im, at_re, at_im)
        if k >= 5:
            place = 64 + 32 * (k - 5)
            pack_ref[place : place + 16, :] = at_re
            pack_ref[place + 16 : place + 32, :] = at_im

    block = iota2((BLOCKS, HALF), 0)
    after = running
    ahead = jnp.where(block >= 1, pltpu.roll(running, 1, 0), 1.0)
    for k in range(3):
        after = after * jnp.where(block < BLOCKS - 2**k, pltpu.roll(after, BLOCKS - 2**k, 0), 1.0)
        ahead = ahead * jnp.where(block >= 2**k, pltpu.roll(ahead, 2**k, 0), 1.0)

    at_re, at_im = jnp.ones_like(power_re), jnp.zeros_like(power_re)
    for step in range(STEPS):
        power_ref[32 * step : 32 * step + 16, :] = at_re
        power_ref[32 * step + 16 : 32 * step + 32, :] = at_im
        at_re, at_im = cmul(at_re, at_im, power_re, power_im)

    def wide(place):
        return jnp.broadcast_to(pack_ref[place : place + 1, lanes], (BLOCKS, HALF))

    for h in range(2):
        lanes = slice(HALF * h, HALF * h + HALF)
        for j in range(NDIM):
            out_re, out_im = after, jnp.zeros_like(after)
            in_re, in_im = cmul(ahead * wide(32 + j), ahead * wide(48 + j), wide(j), wide(16 + j))
            for k in range(3):
                far_re, far_im = wide(64 + 32 * k + j), wide(80 + 32 * k + j)
                chosen = (block // 2**k) % 2 == 1
                on_re, on_im = cmul(in_re, in_im, far_re, far_im)
                in_re, in_im = jnp.where(chosen, on_re, in_re), jnp.where(chosen, on_im, in_im)
                on_re, on_im = cmul(out_re, out_im, far_re, far_im)
                out_re, out_im = jnp.where(chosen, out_re, on_re), jnp.where(chosen, out_im, on_im)
            leave_ref[16 * j : 16 * j + 8, lanes] = out_re
            leave_ref[16 * j + 8 : 16 * j + 16, lanes] = out_im
            enter_ref[16 * j : 16 * j + 8, lanes] = in_re
            enter_ref[16 * j + 8 : 16 * j + 16, lanes] = in_im


def local_kernel(
    stats_ref,
    sums_ref,
    squares_ref,
    placed_ref,
    back_ref,
    pack_ref,
    leave_ref,
    power_ref,
    message_ref,
    scaled_ref,
    summary,
):
    me = lax.axis_index("span")
    before = jnp.zeros((8, WIDTH), f32)
    for i in range(SPANS):
        before += jnp.where(i < me, stats_ref[8 * i : 8 * i + 8, :], 0.0)

    groups = as_bf16(iota2((WIDTH, WIDTH), 0) // GROUP == iota2((WIDTH, WIDTH), 1) // GROUP)
    cum_sum = dot_parts(sums_ref[...] + before[0:1], groups)
    cum_sq = dot_parts(squares_ref[...] + before[1:2], groups)
    position = time_of(iota2((LENGTH, WIDTH), 0)) + me * LENGTH + 1
    share = 1.0 / (position * GROUP).astype(f32)
    average = cum_sum * share
    spread = cum_sq * share - average * average
    inverse = lax.rsqrt(spread + norm_eps)
    normed = (placed_ref[...] - average) * inverse * pack_ref[200:201, :] + pack_ref[208:209, :]
    back = back_ref[...]
    scaled_ref[...] = normed * jnp.concatenate([back, back], axis=1)

    for h in range(2):
        lanes = slice(HALF * h, HALF * h + HALF)
        for first in range(0, NDIM, CHUNK):

            u = scaled_ref[LENGTH - BLOCKS : LENGTH, lanes]
            ends = [u] * CHUNK + [u * 0.0] * CHUNK
            for step in range(1, STEPS):
                row = LENGTH - BLOCKS * (step + 1)
                u = scaled_ref[row : row + BLOCKS, lanes]
                for n in range(2 * CHUNK):
                    place = 32 * step + 16 * (n // CHUNK) + first + n % CHUNK
                    ends[n] = ends[n] + u * power_ref[place : place + 1, lanes]
            for n in range(CHUNK):
                j = first + n
                end_re, end_im = cmul(
                    ends[n],
                    ends[CHUNK + n],
                    leave_ref[16 * j : 16 * j + 8, lanes],
                    leave_ref[16 * j + 8 : 16 * j + 16, lanes],
                )
                summary[j : j + 1, lanes] = jnp.sum(end_re, axis=0, keepdims=True)
                summary[16 + j : 17 + j, lanes] = jnp.sum(end_im, axis=0, keepdims=True)
    sent = summary[...].astype(bf16)
    for i in range(SPANS):
        message_ref[32 * i : 32 * i + 32, :] = sent


def within_kernel(scaled_ref, retained_ref, pack_ref, mixed):
    block = iota2((BLOCKS, HALF), 0)
    running = retained_ref[LENGTH - BLOCKS : LENGTH, :]
    spans = [running]
    for k in range(2):
        reach = spans[-1]
        shifted = jnp.where(block >= 2**k, pltpu.roll(reach, 2**k, 0), 1.0)
        spans.append(reach * shifted)
    spans = [jnp.where(block >= 2**k, spans[k], 0.0) for k in range(3)]

    def wide(place, lanes):
        return jnp.broadcast_to(pack_ref[place : place + 1, lanes], (BLOCKS, HALF))

    for h in range(2):
        lanes = slice(HALF * h, HALF * h + HALF)
        for first in range(0, NDIM, CHUNK):
            js = range(first, first + CHUNK)
            re_of = [wide(j, lanes) for j in js]
            im_of = [wide(16 + j, lanes) for j in js]

            def end_on(step, held):
                u = scaled_ref[pl.ds(pl.multiple_of(step * BLOCKS, BLOCKS), BLOCKS), lanes]
                following = []
                for n in range(CHUNK):
                    re, im = held[2 * n], held[2 * n + 1]
                    following.append(re * re_of[n] - im * im_of[n] + u)
                    following.append(re * im_of[n] + im * re_of[n])
                return tuple(following)

            u0 = scaled_ref[0:BLOCKS, lanes]
            u1 = scaled_ref[BLOCKS : 2 * BLOCKS, lanes]
            begin = []
            for n in range(CHUNK):
                begin += [u0 * re_of[n] + u1, u0 * im_of[n]]
            ends = lax.fori_loop(2, STEPS, end_on, tuple(begin), unroll=3)
            begin = []
            for n, j in enumerate(js):
                re, im = running * ends[2 * n], running * ends[2 * n + 1]
                for k in range(3):
                    add_re, add_im = cmul(
                        pltpu.roll(re, 2**k, 0),
                        pltpu.roll(im, 2**k, 0),
                        wide(64 + 32 * k + j, lanes),
                        wide(80 + 32 * k + j, lanes),
                    )
                    re, im = re + spans[k] * add_re, im + spans[k] * add_im
                begin.append(jnp.where(block >= 1, pltpu.roll(re, 1, 0), 0.0))
                begin.append(jnp.where(block >= 1, pltpu.roll(im, 1, 0), 0.0))
            out_re = [wide(32 + j, lanes) for j in js]
            out_im = [wide(48 + j, lanes) for j in js]
            skip = pack_ref[192:200, lanes]

            def step_on(step, held):
                rows = pl.ds(pl.multiple_of(step * BLOCKS, BLOCKS), BLOCKS)
                u = scaled_ref[rows, lanes]
                following = []
                terms = []
                for n in range(CHUNK):
                    re, im = held[2 * n], held[2 * n + 1]
                    next_re = re * re_of[n] - im * im_of[n] + u
                    next_im = re * im_of[n] + im * re_of[n]
                    following += [next_re, next_im]
                    terms.append(out_re[n] * next_re - out_im[n] * next_im)
                while len(terms) > 1:
                    terms = [terms[i] + terms[i + 1] for i in range(0, len(terms), 2)]
                if first == 0:
                    mixed[rows, lanes] = terms[0] + skip * u
                else:
                    mixed[rows, lanes] += terms[0]
                return tuple(following)

            lax.fori_loop(0, STEPS, step_on, tuple(begin), unroll=2)


def finish_kernel(
    message_ref,
    stats_ref,
    mixed_ref,
    retained_ref,
    pack_ref,
    enter_ref,
    power_ref,
    weight_ref,
    give_ref,
    keep_ref,
    entering,
    mixed,
):
    me = lax.axis_index("span")
    core = lax.axis_index("tensor") % 2
    far_re, far_im = pack_ref[160:176, :], pack_ref[176:192, :]

    def turn(i, held):
        kept = stats_ref[pl.ds(i * 8 + 2, 1), :]
        piece = message_ref[pl.ds(pl.multiple_of(i * 32, 32), 32), :].astype(f32)
        re, im = cmul(held[0], held[1], far_re, far_im)
        return re * kept + piece[:16], im * kept + piece[16:]

    start = jnp.zeros((NDIM, WIDTH), f32)
    state_re, state_im = lax.fori_loop(0, me, turn, (start, start))
    entering[0:16, :] = state_re
    entering[16:32, :] = state_im

    for h in range(2):
        lanes = slice(HALF * h, HALF * h + HALF)
        for first in range(0, NDIM, CHUNK):
            held = []
            for j in range(first, first + CHUNK):
                held.append(
                    cmul(
                        jnp.broadcast_to(entering[j : j + 1, lanes], (BLOCKS, HALF)),
                        jnp.broadcast_to(entering[16 + j : 17 + j, lanes], (BLOCKS, HALF)),
                        enter_ref[16 * j : 16 * j + 8, lanes],
                        enter_ref[16 * j + 8 : 16 * j + 16, lanes],
                    )
                )
            for step in range(STEPS):
                rows = slice(BLOCKS * step, BLOCKS * step + BLOCKS)
                terms = [
                    re * power_ref[32 * step + first + n : 32 * step + first + n + 1, lanes]
                    - im * power_ref[32 * step + 16 + first + n : 32 * step + 17 + first + n, lanes]
                    for n, (re, im) in enumerate(held)
                ]
                while len(terms) > 1:
                    terms = [terms[i] + terms[i + 1] for i in range(0, len(terms), 2)]
                so_far = mixed_ref[rows, lanes] if first == 0 else mixed[rows, lanes]
                mixed[rows, lanes] = so_far + terms[0]

    retained = retained_ref[...]
    ema = jnp.concatenate([retained, retained], axis=1) * mixed[...]
    active = (ema / (1.0 + jnp.exp(-ema))).astype(bf16)
    slot = iota2((LENGTH, LENGTH), 0)
    wanted = (slot + (1 - core) * HALF) % LENGTH
    chosen = as_bf16(time_of(iota2((LENGTH, LENGTH), 1)) == wanted)
    ordered = dot(chosen, active).astype(bf16)
    product = dot(ordered, weight_ref[...]).astype(bf16)
    give_ref[...] = product[:HALF]
    keep_ref[...] = product[HALF:]


def norm_kernel(parts_ref, gain_ref, out_ref):
    total = parts_ref[0:16, :].astype(f32)
    for i in range(1, 8):
        total += parts_ref[16 * i : 16 * i + 16, :].astype(f32)
    squares = jnp.mean(total * total, axis=1, keepdims=True)
    normed = (total * lax.rsqrt(squares + scale_eps) * gain_ref[...]).astype(bf16)
    for i in range(8):
        out_ref[16 * i : 16 * i + 16, :] = normed


def own_kernel(shared_ref, weight_ref, out_ref):
    out_ref[...] = dot(shared_ref[...], weight_ref[...]).astype(bf16)


def other_kernel(shared_ref, weight_ref, own_ref, out_ref):
    core = lax.axis_index("tensor") % 2
    other = dot(shared_ref[...], weight_ref[...]).astype(bf16)
    out_ref[pl.ds(pl.multiple_of(core * HALF, HALF), HALF), :] = own_ref[...]
    out_ref[pl.ds(pl.multiple_of((1 - core) * HALF, HALF), HALF), :] = other


def call(kernel, count, shapes, scratch=(), space=VMEM, limit=32, cost=None):
    single = len(shapes) == 1
    made = [jax.ShapeDtypeStruct(s, d) for s, d in shapes]
    return pl.pallas_call(
        kernel,
        out_shape=made[0] if single else made,
        in_specs=[space] * count,
        out_specs=VMEM if single else [VMEM] * len(shapes),
        scratch_shapes=list(scratch),
        compiler_params=pltpu.CompilerParams(vmem_limit_bytes=limit * 2**20),
        cost_estimate=cost,
    )


def shards(
    tokens,
    retain,
    norm_gain,
    norm_bias,
    decay_rate,
    ema_angle,
    ema_input,
    ema_output,
    ema_skip,
    shared_weight,
    shared_gain,
    output_weight,
):
    retain = retain.reshape(1, LENGTH)
    with jax.named_scope("stats"):
        own = call(
            stats_kernel,
            2,
            [((8 * SPANS, WIDTH), f32)],
            limit=16,
        )(tokens, retain)
        stats = lax.all_to_all(own, "span", 0, 0, tiled=True)
    with jax.named_scope("local"):
        sums, squares, placed, retained, back, pack, leave, enter, power = call(
            prepare_kernel,
            9,
            [((LENGTH, WIDTH), f32)] * 3
            + [((LENGTH, HALF), f32)] * 2
            + [((216, WIDTH), f32)]
            + [((2 * NDIM * BLOCKS, WIDTH), f32)] * 2
            + [((2 * NDIM * STEPS, WIDTH), f32)],
            limit=16,
            cost=pl.CostEstimate(flops=2 * 10**9, bytes_accessed=2**22, transcendentals=0),
        )(
            tokens,
            retain,
            decay_rate,
            ema_angle,
            ema_input,
            ema_output,
            ema_skip.reshape(1, WIDTH),
            norm_gain.reshape(1, WIDTH),
            norm_bias.reshape(1, WIDTH),
        )
        message, scaled = call(
            local_kernel,
            8,
            [((32 * SPANS, WIDTH), bf16), ((LENGTH, WIDTH), f32)],
            [pltpu.VMEM((32, WIDTH), f32)],
            limit=16,
        )(stats, sums, squares, placed, back, pack, leave, power)
        message = lax.all_to_all(message, "span", 0, 0, tiled=True)
        mixed = call(
            within_kernel,
            3,
            [((LENGTH, WIDTH), f32)],
            limit=16,
            cost=pl.CostEstimate(flops=2 * 10**9, bytes_accessed=2**22, transcendentals=0),
        )(scaled, retained, pack)
    with jax.named_scope("finish"):
        width = shared_weight.shape[1]
        give, keep = call(
            finish_kernel,
            8,
            [((HALF, width), bf16), ((HALF, width), bf16)],
            [pltpu.VMEM((32, WIDTH), f32), pltpu.VMEM((LENGTH, WIDTH), f32)],
            limit=16,
        )(message, stats, mixed, retained, pack, enter, power, shared_weight)
    with jax.named_scope("shared"):
        swap = [(i, i ^ 1) for i in range(16)]
        taken = lax.ppermute(give, "tensor", swap)
        pair = (taken.astype(f32) + keep.astype(f32)).astype(bf16)
        groups = [[core + 2 * z for z in range(8)] for core in range(2)]
        parts = lax.all_to_all(pair, "tensor", 0, 0, tiled=True, axis_index_groups=groups)
        copies = call(norm_kernel, 2, [((HALF, width), bf16)])(parts, shared_gain.reshape(1, width))
    with jax.named_scope("output"):
        half = lax.all_to_all(copies, "tensor", 0, 0, tiled=True, axis_index_groups=groups)
        other = lax.ppermute(half, "tensor", swap)
        own = call(
            own_kernel,
            2,
            [((HALF, WIDTH), bf16)],
            limit=16,
            cost=pl.CostEstimate(flops=10**9, bytes_accessed=2**20, transcendentals=0),
        )(half, output_weight)
        return call(other_kernel, 3, [((LENGTH, WIDTH), bf16)], limit=16)(
            other, output_weight, own
        )


def solution(mesh):
    in_specs = (
        P("span", "tensor"),
        P("span"),
        P("tensor"),
        P("tensor"),
        P(None, "tensor"),
        P(None, "tensor"),
        P(None, "tensor"),
        P(None, None, "tensor"),
        P("tensor"),
        P("tensor", None),
        P(),
        P(None, "tensor"),
    )
    out_specs = P("span", "tensor")
    return jax.shard_map(shards, mesh=mesh, in_specs=in_specs, out_specs=out_specs, check_vma=False)
```

```python
import functools

import jax
import jax.numpy as jnp
from jax import lax
from jax.experimental import pallas as pl
from jax.experimental.pallas import tpu as pltpu
from jax.sharding import PartitionSpec as P

GROUP = 64
SPANS = 16
LENGTH = 256
WIDTH = 256
NDIM = 16
BLOCKS = 8
STEPS = 32
HALF = 128
CHUNK = 8

norm_eps = 1e-05
scale_eps = 1e-06

f32 = jnp.float32
bf16 = jnp.bfloat16
VMEM = pl.BlockSpec(memory_space=pltpu.VMEM)
HBM = pl.BlockSpec(memory_space=pltpu.HBM)


def dot(a, b):
    return lax.dot_general(a, b, (((1,), (0,)), ((), ())), preferred_element_type=f32)


def iota2(shape, axis):
    return lax.broadcasted_iota(jnp.int32, shape, axis)


def time_of(row):
    return (row % BLOCKS) * STEPS + row // BLOCKS


def as_bf16(mask):
    return jnp.where(mask, 1.0, 0.0).astype(bf16)


def group_matrix():
    return as_bf16(iota2((WIDTH, WIDTH), 0) // GROUP == iota2((WIDTH, WIDTH), 1) // GROUP)


def dot_parts(a, b):
    rows = a.shape[0]
    high = a.astype(bf16).astype(f32)
    rest = a - high
    middle = rest.astype(bf16).astype(f32)
    parts = jnp.concatenate([high, middle, rest - middle], axis=0).astype(bf16)
    product = dot(parts, b)
    return product[:rows] + product[rows : 2 * rows] + product[2 * rows :]


def cmul(ar, ai, br, bi):
    return ar * br - ai * bi, ar * bi + ai * br


def stats_kernel(tokens_hbm, retain_hbm, out_ref, tokens_ref, retain_ref, arrived):
    copies = (
        pltpu.make_async_copy(tokens_hbm, tokens_ref, arrived.at[0]),
        pltpu.make_async_copy(retain_hbm, retain_ref, arrived.at[1]),
    )
    for copy in copies:
        copy.start()
    for copy in copies:
        copy.wait()
    values = tokens_ref[...].astype(f32)
    total = jnp.sum(values, axis=0, keepdims=True)
    squares = jnp.sum(values * values, axis=0, keepdims=True)
    kept = retain_ref[...]
    size = LENGTH
    while size > 1:
        size //= 2
        kept = kept[:, :size] * kept[:, size:]
    row = iota2((8, WIDTH), 0)
    block = jnp.where(row == 0, total, jnp.where(row == 1, squares, kept))
    for i in range(SPANS):
        out_ref[8 * i : 8 * i + 8, :] = block


def prepare_kernel(
    tokens_ref,
    retain_ref,
    decay_ref,
    angle_ref,
    input_ref,
    output_ref,
    skip_ref,
    gain_ref,
    bias_ref,
    sums_ref,
    squares_ref,
    placed_ref,
    retained_ref,
    back_ref,
    pack_ref,
    leave_ref,
    enter_ref,
    power_ref,
):
    tokens = tokens_ref[...]
    row = time_of(iota2((LENGTH, LENGTH), 0))
    column = iota2((LENGTH, LENGTH), 1)
    upto = as_bf16(column <= row)
    values = tokens.astype(f32)
    squares = values * values
    high = squares.astype(bf16)
    low = (squares - high.astype(f32)).astype(bf16)
    groups = group_matrix()
    sums_ref[...] = dot_parts(dot(upto, tokens), groups)
    squares_ref[...] = dot_parts(dot(upto, high) + dot(upto, low), groups)
    placed_ref[...] = dot(as_bf16(column == row), tokens)

    factor = jnp.sum(jnp.where(column == row, retain_ref[...], 0.0), axis=1, keepdims=True)
    running = jnp.ones((BLOCKS, HALF), f32)
    for step in range(STEPS):
        rows = slice(BLOCKS * step, BLOCKS * step + BLOCKS)
        running = running * factor[rows]
        retained_ref[rows, :] = running
        back_ref[rows, :] = 1.0 / running

    decay = decay_ref[...]
    size = jnp.exp(-decay)
    power_re = size * jnp.cos(angle_ref[...])
    power_im = size * jnp.sin(angle_ref[...])
    weight = (1.0 - size) * input_ref[...]
    pack_ref[0:16, :] = power_re
    pack_ref[16:32, :] = power_im
    pack_ref[32:48, :] = output_ref[0] * weight
    pack_ref[48:64, :] = output_ref[1] * weight
    pack_ref[192:200, :] = jnp.broadcast_to(skip_ref[...], (8, WIDTH))
    pack_ref[200:208, :] = jnp.broadcast_to(gain_ref[...], (8, WIDTH))
    pack_ref[208:216, :] = jnp.broadcast_to(bias_ref[...], (8, WIDTH))
    at_re, at_im = power_re, power_im
    for k in range(1, 9):
        at_re, at_im = cmul(at_re, at_im, at_re, at_im)
        if k >= 5:
            place = 64 + 32 * (k - 5)
            pack_ref[place : place + 16, :] = at_re
            pack_ref[place + 16 : place + 32, :] = at_im

    block = iota2((BLOCKS, HALF), 0)
    after = running
    ahead = jnp.where(block >= 1, pltpu.roll(running, 1, 0), 1.0)
    for k in range(3):
        after = after * jnp.where(block < BLOCKS - 2**k, pltpu.roll(after, BLOCKS - 2**k, 0), 1.0)
        ahead = ahead * jnp.where(block >= 2**k, pltpu.roll(ahead, 2**k, 0), 1.0)

    at_re, at_im = jnp.ones_like(power_re), jnp.zeros_like(power_re)
    for step in range(STEPS):
        power_ref[32 * step : 32 * step + 16, :] = at_re
        power_ref[32 * step + 16 : 32 * step + 32, :] = at_im
        at_re, at_im = cmul(at_re, at_im, power_re, power_im)

    def wide(place):
        return jnp.broadcast_to(pack_ref[place : place + 1, lanes], (BLOCKS, HALF))

    for h in range(2):
        lanes = slice(HALF * h, HALF * h + HALF)
        for j in range(NDIM):
            out_re, out_im = after, jnp.zeros_like(after)
            in_re, in_im = cmul(ahead * wide(32 + j), ahead * wide(48 + j), wide(j), wide(16 + j))
            for k in range(3):
                far_re, far_im = wide(64 + 32 * k + j), wide(80 + 32 * k + j)
                chosen = (block // 2**k) % 2 == 1
                on_re, on_im = cmul(in_re, in_im, far_re, far_im)
                in_re, in_im = jnp.where(chosen, on_re, in_re), jnp.where(chosen, on_im, in_im)
                on_re, on_im = cmul(out_re, out_im, far_re, far_im)
                out_re, out_im = jnp.where(chosen, out_re, on_re), jnp.where(chosen, out_im, on_im)
            leave_ref[16 * j : 16 * j + 8, lanes] = out_re
            leave_ref[16 * j + 8 : 16 * j + 16, lanes] = out_im
            enter_ref[16 * j : 16 * j + 8, lanes] = in_re
            enter_ref[16 * j + 8 : 16 * j + 16, lanes] = in_im


def local_kernel(
    stats_ref,
    sums_ref,
    squares_ref,
    placed_ref,
    back_ref,
    pack_ref,
    leave_ref,
    power_ref,
    message_ref,
    scaled_ref,
    ends_ref,
    summary,
):
    me = lax.axis_index("span")
    before = jnp.zeros((8, WIDTH), f32)
    for i in range(SPANS):
        before += jnp.where(i < me, stats_ref[8 * i : 8 * i + 8, :], 0.0)

    before = dot_parts(before, group_matrix())
    cum_sum = sums_ref[...] + before[0:1]
    cum_sq = squares_ref[...] + before[1:2]
    position = time_of(iota2((LENGTH, WIDTH), 0)) + me * LENGTH + 1
    share = 1.0 / (position * GROUP).astype(f32)
    average = cum_sum * share
    spread = cum_sq * share - average * average
    inverse = lax.rsqrt(spread + norm_eps)
    normed = (placed_ref[...] - average) * inverse * pack_ref[200:201, :] + pack_ref[208:209, :]
    back = back_ref[...]
    scaled_ref[...] = normed * jnp.concatenate([back, back], axis=1)

    for h in range(2):
        lanes = slice(HALF * h, HALF * h + HALF)
        for first in range(0, NDIM, CHUNK):

            u = scaled_ref[LENGTH - BLOCKS : LENGTH, lanes]
            ends = [u] * CHUNK + [u * 0.0] * CHUNK
            for step in range(1, STEPS):
                row = LENGTH - BLOCKS * (step + 1)
                u = scaled_ref[row : row + BLOCKS, lanes]
                for n in range(2 * CHUNK):
                    place = 32 * step + 16 * (n // CHUNK) + first + n % CHUNK
                    ends[n] = ends[n] + u * power_ref[place : place + 1, lanes]
            for n in range(CHUNK):
                j = first + n
                ends_ref[16 * j : 16 * j + 8, lanes] = ends[n]
                ends_ref[16 * j + 8 : 16 * j + 16, lanes] = ends[CHUNK + n]
                end_re, end_im = cmul(
                    ends[n],
                    ends[CHUNK + n],
                    leave_ref[16 * j : 16 * j + 8, lanes],
                    leave_ref[16 * j + 8 : 16 * j + 16, lanes],
                )
                summary[j : j + 1, lanes] = jnp.sum(end_re, axis=0, keepdims=True)
                summary[16 + j : 17 + j, lanes] = jnp.sum(end_im, axis=0, keepdims=True)
    sent = summary[...].astype(bf16)
    for i in range(SPANS):
        message_ref[32 * i : 32 * i + 32, :] = sent


def within_kernel(scaled_ref, ends_ref, retained_ref, pack_ref, mixed):
    block = iota2((BLOCKS, HALF), 0)
    running = retained_ref[LENGTH - BLOCKS : LENGTH, :]
    spans = [running]
    for k in range(2):
        reach = spans[-1]
        shifted = jnp.where(block >= 2**k, pltpu.roll(reach, 2**k, 0), 1.0)
        spans.append(reach * shifted)
    spans = [jnp.where(block >= 2**k, spans[k], 0.0) for k in range(3)]

    def wide(place, lanes):
        return jnp.broadcast_to(pack_ref[place : place + 1, lanes], (BLOCKS, HALF))

    for h in range(2):
        lanes = slice(HALF * h, HALF * h + HALF)
        for first in range(0, NDIM, CHUNK):
            js = range(first, first + CHUNK)
            re_of = [wide(j, lanes) for j in js]
            im_of = [wide(16 + j, lanes) for j in js]

            begin = []
            for n, j in enumerate(js):
                re = running * ends_ref[16 * j : 16 * j + 8, lanes]
                im = running * ends_ref[16 * j + 8 : 16 * j + 16, lanes]
                for k in range(3):
                    add_re, add_im = cmul(
                        pltpu.roll(re, 2**k, 0),
                        pltpu.roll(im, 2**k, 0),
                        wide(64 + 32 * k + j, lanes),
                        wide(80 + 32 * k + j, lanes),
                    )
                    re, im = re + spans[k] * add_re, im + spans[k] * add_im
                begin.append(jnp.where(block >= 1, pltpu.roll(re, 1, 0), 0.0))
                begin.append(jnp.where(block >= 1, pltpu.roll(im, 1, 0), 0.0))
            out_re = [wide(32 + j, lanes) for j in js]
            out_im = [wide(48 + j, lanes) for j in js]
            skip = pack_ref[192:200, lanes]

            def step_on(step, held):
                rows = pl.ds(pl.multiple_of(step * BLOCKS, BLOCKS), BLOCKS)
                u = scaled_ref[rows, lanes]
                following = []
                terms = []
                for n in range(CHUNK):
                    re, im = held[2 * n], held[2 * n + 1]
                    next_re = re * re_of[n] - im * im_of[n] + u
                    next_im = re * im_of[n] + im * re_of[n]
                    following += [next_re, next_im]
                    terms.append(out_re[n] * next_re - out_im[n] * next_im)
                while len(terms) > 1:
                    terms = [terms[i] + terms[i + 1] for i in range(0, len(terms), 2)]
                if first == 0:
                    mixed[rows, lanes] = terms[0] + skip * u
                else:
                    mixed[rows, lanes] += terms[0]
                return tuple(following)

            lax.fori_loop(0, STEPS, step_on, tuple(begin), unroll=2)


def finish_kernel(
    message_ref,
    stats_ref,
    mixed_ref,
    retained_ref,
    pack_ref,
    enter_ref,
    power_ref,
    weight_ref,
    give_ref,
    keep_ref,
    entering,
    mixed,
):
    me = lax.axis_index("span")
    core = lax.axis_index("tensor") % 2
    far_re, far_im = pack_ref[160:176, :], pack_ref[176:192, :]

    def turn(i, held):
        kept = stats_ref[pl.ds(i * 8 + 2, 1), :]
        piece = message_ref[pl.ds(pl.multiple_of(i * 32, 32), 32), :].astype(f32)
        re, im = cmul(held[0], held[1], far_re, far_im)
        return re * kept + piece[:16], im * kept + piece[16:]

    start = jnp.zeros((NDIM, WIDTH), f32)
    state_re, state_im = lax.fori_loop(0, me, turn, (start, start))
    entering[0:16, :] = state_re
    entering[16:32, :] = state_im

    for h in range(2):
        lanes = slice(HALF * h, HALF * h + HALF)
        for first in range(0, NDIM, CHUNK):
            held = []
            for j in range(first, first + CHUNK):
                held.append(
                    cmul(
                        jnp.broadcast_to(entering[j : j + 1, lanes], (BLOCKS, HALF)),
                        jnp.broadcast_to(entering[16 + j : 17 + j, lanes], (BLOCKS, HALF)),
                        enter_ref[16 * j : 16 * j + 8, lanes],
                        enter_ref[16 * j + 8 : 16 * j + 16, lanes],
                    )
                )
            for step in range(STEPS):
                rows = slice(BLOCKS * step, BLOCKS * step + BLOCKS)
                terms = [
                    re * power_ref[32 * step + first + n : 32 * step + first + n + 1, lanes]
                    - im * power_ref[32 * step + 16 + first + n : 32 * step + 17 + first + n, lanes]
                    for n, (re, im) in enumerate(held)
                ]
                while len(terms) > 1:
                    terms = [terms[i] + terms[i + 1] for i in range(0, len(terms), 2)]
                so_far = mixed_ref[rows, lanes] if first == 0 else mixed[rows, lanes]
                mixed[rows, lanes] = so_far + terms[0]

    retained = retained_ref[...]
    ema = jnp.concatenate([retained, retained], axis=1) * mixed[...]
    active = (ema / (1.0 + jnp.exp(-ema))).astype(bf16)
    slot = iota2((LENGTH, LENGTH), 0)
    wanted = (slot + (1 - core) * HALF) % LENGTH
    chosen = as_bf16(time_of(iota2((LENGTH, LENGTH), 1)) == wanted)
    ordered = dot(chosen, active).astype(bf16)
    product = dot(ordered, weight_ref[...]).astype(bf16)
    give_ref[...] = product[:HALF]
    keep_ref[...] = product[HALF:]


def norm_kernel(parts_ref, gain_ref, out_ref):
    total = parts_ref[0:16, :].astype(f32)
    for i in range(1, 8):
        total += parts_ref[16 * i : 16 * i + 16, :].astype(f32)
    squares = jnp.mean(total * total, axis=1, keepdims=True)
    normed = (total * lax.rsqrt(squares + scale_eps) * gain_ref[...]).astype(bf16)
    for i in range(8):
        out_ref[16 * i : 16 * i + 16, :] = normed


def half_kernel(own, shared_ref, weight_ref, *refs):
    out_ref, half, done = refs[-3:]
    core = lax.axis_index("tensor") % 2
    side = core if own else 1 - core
    place = pl.multiple_of(side * HALF, HALF)
    half[...] = dot(shared_ref[...], weight_ref[...]).astype(bf16)
    copy = pltpu.make_async_copy(half, out_ref.at[pl.ds(place, HALF), :], done)
    copy.start()
    copy.wait()


def half_call(own, *operands):
    return pl.pallas_call(
        functools.partial(half_kernel, own),
        out_shape=jax.ShapeDtypeStruct((LENGTH, WIDTH), bf16),
        in_specs=[VMEM, VMEM] + [HBM] * (len(operands) - 2),
        out_specs=HBM,
        scratch_shapes=[pltpu.VMEM((HALF, WIDTH), bf16), pltpu.SemaphoreType.DMA],
        input_output_aliases={} if own else {2: 0},
        compiler_params=pltpu.CompilerParams(vmem_limit_bytes=16 * 2**20),
        cost_estimate=pl.CostEstimate(flops=10**9, bytes_accessed=2**20, transcendentals=0),
    )(*operands)


def call(kernel, count, shapes, scratch=(), space=VMEM, limit=32, cost=None):
    single = len(shapes) == 1
    made = [jax.ShapeDtypeStruct(s, d) for s, d in shapes]
    return pl.pallas_call(
        kernel,
        out_shape=made[0] if single else made,
        in_specs=[space] * count,
        out_specs=VMEM if single else [VMEM] * len(shapes),
        scratch_shapes=list(scratch),
        compiler_params=pltpu.CompilerParams(vmem_limit_bytes=limit * 2**20),
        cost_estimate=cost,
    )


def shards(
    tokens,
    retain,
    norm_gain,
    norm_bias,
    decay_rate,
    ema_angle,
    ema_input,
    ema_output,
    ema_skip,
    shared_weight,
    shared_gain,
    output_weight,
):
    retain = retain.reshape(1, LENGTH)
    with jax.named_scope("stats"):
        own = call(
            stats_kernel,
            2,
            [((8 * SPANS, WIDTH), f32)],
            [
                pltpu.VMEM((LENGTH, WIDTH), bf16),
                pltpu.VMEM((1, LENGTH), f32),
                pltpu.SemaphoreType.DMA((2,)),
            ],
            HBM,
            60,
        )(tokens, retain)
        stats = lax.all_to_all(own, "span", 0, 0, tiled=True)
    with jax.named_scope("local"):
        sums, squares, placed, retained, back, pack, leave, enter, power = call(
            prepare_kernel,
            9,
            [((LENGTH, WIDTH), f32)] * 3
            + [((LENGTH, HALF), f32)] * 2
            + [((216, WIDTH), f32)]
            + [((2 * NDIM * BLOCKS, WIDTH), f32)] * 2
            + [((2 * NDIM * STEPS, WIDTH), f32)],
            limit=16,
            cost=pl.CostEstimate(flops=2 * 10**9, bytes_accessed=2**22, transcendentals=0),
        )(
            tokens,
            retain,
            decay_rate,
            ema_angle,
            ema_input,
            ema_output,
            ema_skip.reshape(1, WIDTH),
            norm_gain.reshape(1, WIDTH),
            norm_bias.reshape(1, WIDTH),
        )
        message, scaled, ends = call(
            local_kernel,
            8,
            [
                ((32 * SPANS, WIDTH), bf16),
                ((LENGTH, WIDTH), f32),
                ((2 * NDIM * BLOCKS, WIDTH), f32),
            ],
            [pltpu.VMEM((32, WIDTH), f32)],
            limit=16,
        )(stats, sums, squares, placed, back, pack, leave, power)
        message = lax.all_to_all(message, "span", 0, 0, tiled=True)
        mixed = call(
            within_kernel,
            4,
            [((LENGTH, WIDTH), f32)],
            limit=16,
            cost=pl.CostEstimate(flops=2 * 10**9, bytes_accessed=2**22, transcendentals=0),
        )(scaled, ends, retained, pack)
    with jax.named_scope("finish"):
        width = shared_weight.shape[1]
        give, keep = call(
            finish_kernel,
            8,
            [((HALF, width), bf16), ((HALF, width), bf16)],
            [pltpu.VMEM((32, WIDTH), f32), pltpu.VMEM((LENGTH, WIDTH), f32)],
            limit=16,
        )(message, stats, mixed, retained, pack, enter, power, shared_weight)
    with jax.named_scope("shared"):
        swap = [(i, i ^ 1) for i in range(16)]
        taken = lax.ppermute(give, "tensor", swap)
        pair = (taken.astype(f32) + keep.astype(f32)).astype(bf16)
        groups = [[core + 2 * z for z in range(8)] for core in range(2)]
        parts = lax.all_to_all(pair, "tensor", 0, 0, tiled=True, axis_index_groups=groups)
        copies = call(norm_kernel, 2, [((HALF, width), bf16)])(parts, shared_gain.reshape(1, width))
    with jax.named_scope("output"):
        half = lax.all_to_all(copies, "tensor", 0, 0, tiled=True, axis_index_groups=groups)
        other = lax.ppermute(half, "tensor", swap)
        out = half_call(True, half, output_weight)
        return half_call(False, other, output_weight, out)


def solution(mesh):
    in_specs = (
        P("span", "tensor"),
        P("span"),
        P("tensor"),
        P("tensor"),
        P(None, "tensor"),
        P(None, "tensor"),
        P(None, "tensor"),
        P(None, None, "tensor"),
        P("tensor"),
        P("tensor", None),
        P(),
        P(None, "tensor"),
    )
    out_specs = P("span", "tensor")
    return jax.shard_map(shards, mesh=mesh, in_specs=in_specs, out_specs=out_specs, check_vma=False)
```

```python
import functools

import jax
import jax.numpy as jnp
from jax import lax
from jax.experimental import pallas as pl
from jax.experimental.pallas import tpu as pltpu
from jax.sharding import PartitionSpec as P

GROUP = 64
SPANS = 16
LENGTH = 256
WIDTH = 256
NDIM = 16
BLOCKS = 8
STEPS = 32
HALF = 128
CHUNK = 8

norm_eps = 1e-05
scale_eps = 1e-06

f32 = jnp.float32
bf16 = jnp.bfloat16
VMEM = pl.BlockSpec(memory_space=pltpu.VMEM)
HBM = pl.BlockSpec(memory_space=pltpu.HBM)


def dot(a, b):
    return lax.dot_general(a, b, (((1,), (0,)), ((), ())), preferred_element_type=f32)


def iota2(shape, axis):
    return lax.broadcasted_iota(jnp.int32, shape, axis)


def time_of(row):
    return (row % BLOCKS) * STEPS + row // BLOCKS


def as_bf16(mask):
    return jnp.where(mask, 1.0, 0.0).astype(bf16)


def group_matrix():
    return as_bf16(iota2((WIDTH, WIDTH), 0) // GROUP == iota2((WIDTH, WIDTH), 1) // GROUP)


def dot_parts(a, b):
    rows = a.shape[0]
    high = a.astype(bf16).astype(f32)
    rest = a - high
    middle = rest.astype(bf16).astype(f32)
    parts = jnp.concatenate([high, middle, rest - middle], axis=0).astype(bf16)
    product = dot(parts, b)
    return product[:rows] + product[rows : 2 * rows] + product[2 * rows :]


def cmul(ar, ai, br, bi):
    return ar * br - ai * bi, ar * bi + ai * br


def stats_kernel(tokens_hbm, retain_hbm, out_ref, tokens_ref, retain_ref, arrived):
    pieces = 4
    size = LENGTH // pieces
    copies = [pltpu.make_async_copy(retain_hbm, retain_ref, arrived.at[pieces])]
    for i in range(pieces):
        rows = pl.ds(i * size, size)
        copies.append(
            pltpu.make_async_copy(tokens_hbm.at[rows, :], tokens_ref.at[rows, :], arrived.at[i])
        )
    for copy in copies:
        copy.start()
    copies[0].wait()
    kept = retain_ref[...]
    kept = kept[:, :HALF] * kept[:, HALF:]
    for k in range(7):
        kept = kept * pltpu.roll(kept, 2**k, 1)
    kept = jnp.concatenate([kept, kept], axis=1)
    total = squares = 0.0
    for i in range(pieces):
        copies[1 + i].wait()
        values = tokens_ref[size * i : size * i + size, :].astype(f32)
        total = total + jnp.sum(values, axis=0, keepdims=True)
        squares = squares + jnp.sum(values * values, axis=0, keepdims=True)
    row = iota2((8, WIDTH), 0)
    block = jnp.where(row == 0, total, jnp.where(row == 1, squares, kept))
    for i in range(SPANS):
        out_ref[8 * i : 8 * i + 8, :] = block


def prepare_kernel(
    tokens_ref,
    retain_ref,
    decay_ref,
    angle_ref,
    input_ref,
    output_ref,
    skip_ref,
    gain_ref,
    bias_ref,
    sums_ref,
    squares_ref,
    placed_ref,
    retained_ref,
    back_ref,
    pack_ref,
    leave_ref,
    enter_ref,
    power_ref,
):
    tokens = tokens_ref[...]
    row = time_of(iota2((LENGTH, LENGTH), 0))
    column = iota2((LENGTH, LENGTH), 1)
    upto = as_bf16(column <= row)
    values = tokens.astype(f32)
    squares = values * values
    high = squares.astype(bf16)
    low = (squares - high.astype(f32)).astype(bf16)
    groups = group_matrix()
    sums_ref[...] = dot_parts(dot(upto, tokens), groups)
    squares_ref[...] = dot_parts(dot(upto, high) + dot(upto, low), groups)
    placed_ref[...] = dot(as_bf16(column == row), tokens)

    factor = jnp.sum(jnp.where(column == row, retain_ref[...], 0.0), axis=1, keepdims=True)
    running = jnp.ones((BLOCKS, HALF), f32)
    for step in range(STEPS):
        rows = slice(BLOCKS * step, BLOCKS * step + BLOCKS)
        running = running * factor[rows]
        retained_ref[rows, :] = running
        back_ref[rows, :] = 1.0 / running

    decay = decay_ref[...]
    size = jnp.exp(-decay)
    power_re = size * jnp.cos(angle_ref[...])
    power_im = size * jnp.sin(angle_ref[...])
    weight = (1.0 - size) * input_ref[...]
    pack_ref[0:16, :] = power_re
    pack_ref[16:32, :] = power_im
    pack_ref[32:48, :] = output_ref[0] * weight
    pack_ref[48:64, :] = output_ref[1] * weight
    pack_ref[192:200, :] = jnp.broadcast_to(skip_ref[...], (8, WIDTH))
    pack_ref[200:208, :] = jnp.broadcast_to(gain_ref[...], (8, WIDTH))
    pack_ref[208:216, :] = jnp.broadcast_to(bias_ref[...], (8, WIDTH))
    at_re, at_im = power_re, power_im
    for k in range(1, 9):
        at_re, at_im = cmul(at_re, at_im, at_re, at_im)
        if k >= 5:
            place = 64 + 32 * (k - 5)
            pack_ref[place : place + 16, :] = at_re
            pack_ref[place + 16 : place + 32, :] = at_im

    block = iota2((BLOCKS, HALF), 0)
    after = running
    ahead = jnp.where(block >= 1, pltpu.roll(running, 1, 0), 1.0)
    for k in range(3):
        after = after * jnp.where(block < BLOCKS - 2**k, pltpu.roll(after, BLOCKS - 2**k, 0), 1.0)
        ahead = ahead * jnp.where(block >= 2**k, pltpu.roll(ahead, 2**k, 0), 1.0)

    at_re, at_im = jnp.ones_like(power_re), jnp.zeros_like(power_re)
    for step in range(STEPS):
        power_ref[32 * step : 32 * step + 16, :] = at_re
        power_ref[32 * step + 16 : 32 * step + 32, :] = at_im
        at_re, at_im = cmul(at_re, at_im, power_re, power_im)

    def wide(place):
        return jnp.broadcast_to(pack_ref[place : place + 1, lanes], (BLOCKS, HALF))

    for h in range(2):
        lanes = slice(HALF * h, HALF * h + HALF)
        for j in range(NDIM):
            out_re, out_im = after, jnp.zeros_like(after)
            in_re, in_im = cmul(ahead * wide(32 + j), ahead * wide(48 + j), wide(j), wide(16 + j))
            for k in range(3):
                far_re, far_im = wide(64 + 32 * k + j), wide(80 + 32 * k + j)
                chosen = (block // 2**k) % 2 == 1
                on_re, on_im = cmul(in_re, in_im, far_re, far_im)
                in_re, in_im = jnp.where(chosen, on_re, in_re), jnp.where(chosen, on_im, in_im)
                on_re, on_im = cmul(out_re, out_im, far_re, far_im)
                out_re, out_im = jnp.where(chosen, out_re, on_re), jnp.where(chosen, out_im, on_im)
            leave_ref[16 * j : 16 * j + 8, lanes] = out_re
            leave_ref[16 * j + 8 : 16 * j + 16, lanes] = out_im
            enter_ref[16 * j : 16 * j + 8, lanes] = in_re
            enter_ref[16 * j + 8 : 16 * j + 16, lanes] = in_im


def local_kernel(
    stats_ref,
    sums_ref,
    squares_ref,
    placed_ref,
    back_ref,
    pack_ref,
    leave_ref,
    power_ref,
    message_ref,
    scaled_ref,
    ends_ref,
    summary,
):
    me = lax.axis_index("span")
    before = jnp.zeros((8, WIDTH), f32)
    for i in range(SPANS):
        before += jnp.where(i < me, stats_ref[8 * i : 8 * i + 8, :], 0.0)

    before = dot_parts(before, group_matrix())
    cum_sum = sums_ref[...] + before[0:1]
    cum_sq = squares_ref[...] + before[1:2]
    position = time_of(iota2((LENGTH, WIDTH), 0)) + me * LENGTH + 1
    share = 1.0 / (position * GROUP).astype(f32)
    average = cum_sum * share
    spread = cum_sq * share - average * average
    inverse = lax.rsqrt(spread + norm_eps)
    normed = (placed_ref[...] - average) * inverse * pack_ref[200:201, :] + pack_ref[208:209, :]
    back = back_ref[...]
    scaled_ref[...] = normed * jnp.concatenate([back, back], axis=1)

    for h in range(2):
        lanes = slice(HALF * h, HALF * h + HALF)
        for first in range(0, NDIM, CHUNK):

            u = scaled_ref[LENGTH - BLOCKS : LENGTH, lanes]
            ends = [u] * CHUNK + [u * 0.0] * CHUNK
            for step in range(1, STEPS):
                row = LENGTH - BLOCKS * (step + 1)
                u = scaled_ref[row : row + BLOCKS, lanes]
                for n in range(2 * CHUNK):
                    place = 32 * step + 16 * (n // CHUNK) + first + n % CHUNK
                    ends[n] = ends[n] + u * power_ref[place : place + 1, lanes]
            for n in range(CHUNK):
                j = first + n
                ends_ref[16 * j : 16 * j + 8, lanes] = ends[n]
                ends_ref[16 * j + 8 : 16 * j + 16, lanes] = ends[CHUNK + n]
                end_re, end_im = cmul(
                    ends[n],
                    ends[CHUNK + n],
                    leave_ref[16 * j : 16 * j + 8, lanes],
                    leave_ref[16 * j + 8 : 16 * j + 16, lanes],
                )
                summary[j : j + 1, lanes] = jnp.sum(end_re, axis=0, keepdims=True)
                summary[16 + j : 17 + j, lanes] = jnp.sum(end_im, axis=0, keepdims=True)
    sent = summary[...].astype(bf16)
    for i in range(SPANS):
        message_ref[32 * i : 32 * i + 32, :] = sent


def within_kernel(scaled_ref, ends_ref, retained_ref, pack_ref, mixed):
    block = iota2((BLOCKS, HALF), 0)
    running = retained_ref[LENGTH - BLOCKS : LENGTH, :]
    spans = [running]
    for k in range(2):
        reach = spans[-1]
        shifted = jnp.where(block >= 2**k, pltpu.roll(reach, 2**k, 0), 1.0)
        spans.append(reach * shifted)
    spans = [jnp.where(block >= 2**k, spans[k], 0.0) for k in range(3)]

    def wide(place, lanes):
        return jnp.broadcast_to(pack_ref[place : place + 1, lanes], (BLOCKS, HALF))

    for h in range(2):
        lanes = slice(HALF * h, HALF * h + HALF)
        for first in range(0, NDIM, CHUNK):
            js = range(first, first + CHUNK)
            re_of = [wide(j, lanes) for j in js]
            im_of = [wide(16 + j, lanes) for j in js]

            begin = []
            for n, j in enumerate(js):
                re = running * ends_ref[16 * j : 16 * j + 8, lanes]
                im = running * ends_ref[16 * j + 8 : 16 * j + 16, lanes]
                for k in range(3):
                    add_re, add_im = cmul(
                        pltpu.roll(re, 2**k, 0),
                        pltpu.roll(im, 2**k, 0),
                        wide(64 + 32 * k + j, lanes),
                        wide(80 + 32 * k + j, lanes),
                    )
                    re, im = re + spans[k] * add_re, im + spans[k] * add_im
                begin.append(jnp.where(block >= 1, pltpu.roll(re, 1, 0), 0.0))
                begin.append(jnp.where(block >= 1, pltpu.roll(im, 1, 0), 0.0))
            out_re = [wide(32 + j, lanes) for j in js]
            out_im = [wide(48 + j, lanes) for j in js]
            skip = pack_ref[192:200, lanes]

            def step_on(step, held):
                rows = pl.ds(pl.multiple_of(step * BLOCKS, BLOCKS), BLOCKS)
                u = scaled_ref[rows, lanes]
                following = []
                terms = []
                for n in range(CHUNK):
                    re, im = held[2 * n], held[2 * n + 1]
                    next_re = re * re_of[n] - im * im_of[n] + u
                    next_im = re * im_of[n] + im * re_of[n]
                    following += [next_re, next_im]
                    terms.append(out_re[n] * next_re - out_im[n] * next_im)
                while len(terms) > 1:
                    terms = [terms[i] + terms[i + 1] for i in range(0, len(terms), 2)]
                if first == 0:
                    mixed[rows, lanes] = terms[0] + skip * u
                else:
                    mixed[rows, lanes] += terms[0]
                return tuple(following)

            lax.fori_loop(0, STEPS, step_on, tuple(begin), unroll=2)


def finish_kernel(
    message_ref,
    stats_ref,
    mixed_ref,
    retained_ref,
    pack_ref,
    enter_ref,
    power_ref,
    weight_ref,
    give_ref,
    active_ref,
    entering,
    mixed,
):
    me = lax.axis_index("span")
    core = lax.axis_index("tensor") % 2
    far_re, far_im = pack_ref[160:176, :], pack_ref[176:192, :]

    def turn(i, held):
        kept = stats_ref[pl.ds(i * 8 + 2, 1), :]
        piece = message_ref[pl.ds(pl.multiple_of(i * 32, 32), 32), :].astype(f32)
        re, im = cmul(held[0], held[1], far_re, far_im)
        return re * kept + piece[:16], im * kept + piece[16:]

    start = jnp.zeros((NDIM, WIDTH), f32)
    state_re, state_im = lax.fori_loop(0, me, turn, (start, start))
    entering[0:16, :] = state_re
    entering[16:32, :] = state_im

    for h in range(2):
        lanes = slice(HALF * h, HALF * h + HALF)
        for first in range(0, NDIM, CHUNK):
            held = []
            for j in range(first, first + CHUNK):
                held.append(
                    cmul(
                        jnp.broadcast_to(entering[j : j + 1, lanes], (BLOCKS, HALF)),
                        jnp.broadcast_to(entering[16 + j : 17 + j, lanes], (BLOCKS, HALF)),
                        enter_ref[16 * j : 16 * j + 8, lanes],
                        enter_ref[16 * j + 8 : 16 * j + 16, lanes],
                    )
                )
            for step in range(STEPS):
                rows = slice(BLOCKS * step, BLOCKS * step + BLOCKS)
                terms = [
                    re * power_ref[32 * step + first + n : 32 * step + first + n + 1, lanes]
                    - im * power_ref[32 * step + 16 + first + n : 32 * step + 17 + first + n, lanes]
                    for n, (re, im) in enumerate(held)
                ]
                while len(terms) > 1:
                    terms = [terms[i] + terms[i + 1] for i in range(0, len(terms), 2)]
                so_far = mixed_ref[rows, lanes] if first == 0 else mixed[rows, lanes]
                mixed[rows, lanes] = so_far + terms[0]

    retained = retained_ref[...]
    ema = jnp.concatenate([retained, retained], axis=1) * mixed[...]
    active = (ema / (1.0 + jnp.exp(-ema))).astype(bf16)
    active_ref[...] = active
    give_ref[...] = half_product(1 - core, active, weight_ref[...])


def half_product(side, active, weight):
    wanted = iota2((HALF, LENGTH), 0) + side * HALF
    chosen = as_bf16(time_of(iota2((HALF, LENGTH), 1)) == wanted)
    return dot(dot(chosen, active).astype(bf16), weight).astype(bf16)


def keep_kernel(active_ref, weight_ref, keep_ref):
    core = lax.axis_index("tensor") % 2
    keep_ref[...] = half_product(core, active_ref[...], weight_ref[...])


def norm_kernel(parts_ref, gain_ref, out_ref):
    total = parts_ref[0:16, :].astype(f32)
    for i in range(1, 8):
        total += parts_ref[16 * i : 16 * i + 16, :].astype(f32)
    squares = jnp.mean(total * total, axis=1, keepdims=True)
    normed = (total * lax.rsqrt(squares + scale_eps) * gain_ref[...]).astype(bf16)
    for i in range(8):
        out_ref[16 * i : 16 * i + 16, :] = normed


def half_kernel(own, shared_ref, weight_ref, *refs):
    out_ref, half, done = refs[-3:]
    core = lax.axis_index("tensor") % 2
    side = core if own else 1 - core
    place = pl.multiple_of(side * HALF, HALF)
    half[...] = dot(shared_ref[...], weight_ref[...]).astype(bf16)
    copy = pltpu.make_async_copy(half, out_ref.at[pl.ds(place, HALF), :], done)
    copy.start()
    copy.wait()


def half_call(own, *operands):
    return pl.pallas_call(
        functools.partial(half_kernel, own),
        out_shape=jax.ShapeDtypeStruct((LENGTH, WIDTH), bf16),
        in_specs=[VMEM, VMEM] + [HBM] * (len(operands) - 2),
        out_specs=HBM,
        scratch_shapes=[pltpu.VMEM((HALF, WIDTH), bf16), pltpu.SemaphoreType.DMA],
        input_output_aliases={} if own else {2: 0},
        compiler_params=pltpu.CompilerParams(vmem_limit_bytes=16 * 2**20),
        cost_estimate=pl.CostEstimate(flops=10**9, bytes_accessed=2**20, transcendentals=0),
    )(*operands)


def call(kernel, count, shapes, scratch=(), space=VMEM, limit=32, cost=None):
    single = len(shapes) == 1
    made = [jax.ShapeDtypeStruct(s, d) for s, d in shapes]
    return pl.pallas_call(
        kernel,
        out_shape=made[0] if single else made,
        in_specs=[space] * count,
        out_specs=VMEM if single else [VMEM] * len(shapes),
        scratch_shapes=list(scratch),
        compiler_params=pltpu.CompilerParams(vmem_limit_bytes=limit * 2**20),
        cost_estimate=cost,
    )


def shards(
    tokens,
    retain,
    norm_gain,
    norm_bias,
    decay_rate,
    ema_angle,
    ema_input,
    ema_output,
    ema_skip,
    shared_weight,
    shared_gain,
    output_weight,
):
    retain = retain.reshape(1, LENGTH)
    with jax.named_scope("stats"):
        own = call(
            stats_kernel,
            2,
            [((8 * SPANS, WIDTH), f32)],
            [
                pltpu.VMEM((LENGTH, WIDTH), bf16),
                pltpu.VMEM((1, LENGTH), f32),
                pltpu.SemaphoreType.DMA((5,)),
            ],
            HBM,
            60,
        )(tokens, retain)
        stats = lax.all_to_all(own, "span", 0, 0, tiled=True)
    with jax.named_scope("local"):
        sums, squares, placed, retained, back, pack, leave, enter, power = call(
            prepare_kernel,
            9,
            [((LENGTH, WIDTH), f32)] * 3
            + [((LENGTH, HALF), f32)] * 2
            + [((216, WIDTH), f32)]
            + [((2 * NDIM * BLOCKS, WIDTH), f32)] * 2
            + [((2 * NDIM * STEPS, WIDTH), f32)],
            limit=16,
            cost=pl.CostEstimate(flops=2 * 10**9, bytes_accessed=2**22, transcendentals=0),
        )(
            tokens,
            retain,
            decay_rate,
            ema_angle,
            ema_input,
            ema_output,
            ema_skip.reshape(1, WIDTH),
            norm_gain.reshape(1, WIDTH),
            norm_bias.reshape(1, WIDTH),
        )
        message, scaled, ends = call(
            local_kernel,
            8,
            [
                ((32 * SPANS, WIDTH), bf16),
                ((LENGTH, WIDTH), f32),
                ((2 * NDIM * BLOCKS, WIDTH), f32),
            ],
            [pltpu.VMEM((32, WIDTH), f32)],
            limit=16,
        )(stats, sums, squares, placed, back, pack, leave, power)
        message = lax.all_to_all(message, "span", 0, 0, tiled=True)
        mixed = call(
            within_kernel,
            4,
            [((LENGTH, WIDTH), f32)],
            limit=16,
            cost=pl.CostEstimate(flops=2 * 10**9, bytes_accessed=2**22, transcendentals=0),
        )(scaled, ends, retained, pack)
    with jax.named_scope("finish"):
        width = shared_weight.shape[1]
        give, active = call(
            finish_kernel,
            8,
            [((HALF, width), bf16), ((LENGTH, WIDTH), bf16)],
            [pltpu.VMEM((32, WIDTH), f32), pltpu.VMEM((LENGTH, WIDTH), f32)],
            limit=16,
        )(message, stats, mixed, retained, pack, enter, power, shared_weight)
    with jax.named_scope("shared"):
        swap = [(i, i ^ 1) for i in range(16)]
        taken = lax.ppermute(give, "tensor", swap)
        keep = call(
            keep_kernel,
            2,
            [((HALF, width), bf16)],
            limit=16,
            cost=pl.CostEstimate(flops=10**9, bytes_accessed=2**20, transcendentals=0),
        )(active, shared_weight)
        pair = (taken.astype(f32) + keep.astype(f32)).astype(bf16)
        groups = [[core + 2 * z for z in range(8)] for core in range(2)]
        parts = lax.all_to_all(pair, "tensor", 0, 0, tiled=True, axis_index_groups=groups)
        copies = call(norm_kernel, 2, [((HALF, width), bf16)])(parts, shared_gain.reshape(1, width))
    with jax.named_scope("output"):
        half = lax.all_to_all(copies, "tensor", 0, 0, tiled=True, axis_index_groups=groups)
        other = lax.ppermute(half, "tensor", swap)
        out = half_call(True, half, output_weight)
        return half_call(False, other, output_weight, out)


def solution(mesh):
    in_specs = (
        P("span", "tensor"),
        P("span"),
        P("tensor"),
        P("tensor"),
        P(None, "tensor"),
        P(None, "tensor"),
        P(None, "tensor"),
        P(None, None, "tensor"),
        P("tensor"),
        P("tensor", None),
        P(),
        P(None, "tensor"),
    )
    out_specs = P("span", "tensor")
    return jax.shard_map(shards, mesh=mesh, in_specs=in_specs, out_specs=out_specs, check_vma=False)
```

```python
import functools

import jax
import jax.numpy as jnp
from jax import lax
from jax.experimental import pallas as pl
from jax.experimental.pallas import tpu as pltpu
from jax.sharding import PartitionSpec as P

GROUP = 64
SPANS = 16
LENGTH = 256
WIDTH = 256
NDIM = 16
BLOCKS = 8
STEPS = 32
HALF = 128
CHUNK = 8

norm_eps = 1e-05
scale_eps = 1e-06

f32 = jnp.float32
bf16 = jnp.bfloat16
VMEM = pl.BlockSpec(memory_space=pltpu.VMEM)
HBM = pl.BlockSpec(memory_space=pltpu.HBM)


def dot(a, b):
    return lax.dot_general(a, b, (((1,), (0,)), ((), ())), preferred_element_type=f32)


def iota2(shape, axis):
    return lax.broadcasted_iota(jnp.int32, shape, axis)


def time_of(row):
    return (row % BLOCKS) * STEPS + row // BLOCKS


def as_bf16(mask):
    return jnp.where(mask, 1.0, 0.0).astype(bf16)


def group_matrix():
    return as_bf16(iota2((WIDTH, WIDTH), 0) // GROUP == iota2((WIDTH, WIDTH), 1) // GROUP)


def dot_parts(a, b):
    rows = a.shape[0]
    high = a.astype(bf16).astype(f32)
    rest = a - high
    middle = rest.astype(bf16).astype(f32)
    parts = jnp.concatenate([high, middle, rest - middle], axis=0).astype(bf16)
    product = dot(parts, b)
    return product[:rows] + product[rows : 2 * rows] + product[2 * rows :]


def cmul(ar, ai, br, bi):
    return ar * br - ai * bi, ar * bi + ai * br


def stats_kernel(tokens_hbm, retain_hbm, out_ref, tokens_ref, retain_ref, arrived):
    pieces = 4
    size = LENGTH // pieces
    copies = [pltpu.make_async_copy(retain_hbm, retain_ref, arrived.at[pieces])]
    for i in range(pieces):
        rows = pl.ds(i * size, size)
        copies.append(
            pltpu.make_async_copy(tokens_hbm.at[rows, :], tokens_ref.at[rows, :], arrived.at[i])
        )
    for copy in copies:
        copy.start()
    copies[0].wait()
    kept = retain_ref[...]
    kept = kept[:, :HALF] * kept[:, HALF:]
    for k in range(7):
        kept = kept * pltpu.roll(kept, 2**k, 1)
    kept = jnp.concatenate([kept, kept], axis=1)
    total = squares = 0.0
    for i in range(pieces):
        copies[1 + i].wait()
        values = tokens_ref[size * i : size * i + size, :].astype(f32)
        total = total + jnp.sum(values, axis=0, keepdims=True)
        squares = squares + jnp.sum(values * values, axis=0, keepdims=True)
    row = iota2((8, WIDTH), 0)
    block = jnp.where(row == 0, total, jnp.where(row == 1, squares, kept))
    for i in range(SPANS):
        out_ref[8 * i : 8 * i + 8, :] = block


def prepare_kernel(
    tokens_ref,
    retain_ref,
    decay_ref,
    angle_ref,
    input_ref,
    output_ref,
    skip_ref,
    gain_ref,
    bias_ref,
    sums_ref,
    squares_ref,
    placed_ref,
    retained_ref,
    back_ref,
    pack_ref,
    leave_ref,
    enter_ref,
    power_ref,
):
    tokens = tokens_ref[...]
    row = time_of(iota2((LENGTH, LENGTH), 0))
    column = iota2((LENGTH, LENGTH), 1)
    upto = as_bf16(column <= row)
    values = tokens.astype(f32)
    squares = values * values
    high = squares.astype(bf16)
    low = (squares - high.astype(f32)).astype(bf16)
    groups = group_matrix()
    sums_ref[...] = dot_parts(dot(upto, tokens), groups)
    squares_ref[...] = dot_parts(dot(upto, high) + dot(upto, low), groups)
    placed_ref[...] = dot(as_bf16(column == row), tokens)

    factor = jnp.sum(jnp.where(column == row, retain_ref[...], 0.0), axis=1, keepdims=True)
    running = jnp.ones((BLOCKS, HALF), f32)
    for step in range(STEPS):
        rows = slice(BLOCKS * step, BLOCKS * step + BLOCKS)
        running = running * factor[rows]
        retained_ref[rows, :] = running
        back_ref[rows, :] = 1.0 / running

    decay = decay_ref[...]
    size = jnp.exp(-decay)
    power_re = size * jnp.cos(angle_ref[...])
    power_im = size * jnp.sin(angle_ref[...])
    weight = (1.0 - size) * input_ref[...]
    pack_ref[0:16, :] = power_re
    pack_ref[16:32, :] = power_im
    pack_ref[32:48, :] = output_ref[0] * weight
    pack_ref[48:64, :] = output_ref[1] * weight
    pack_ref[192:200, :] = jnp.broadcast_to(skip_ref[...], (8, WIDTH))
    pack_ref[200:208, :] = jnp.broadcast_to(gain_ref[...], (8, WIDTH))
    pack_ref[208:216, :] = jnp.broadcast_to(bias_ref[...], (8, WIDTH))
    at_re, at_im = power_re, power_im
    for k in range(1, 9):
        at_re, at_im = cmul(at_re, at_im, at_re, at_im)
        if k >= 5:
            place = 64 + 32 * (k - 5)
            pack_ref[place : place + 16, :] = at_re
            pack_ref[place + 16 : place + 32, :] = at_im

    block = iota2((BLOCKS, HALF), 0)
    after = running
    ahead = jnp.where(block >= 1, pltpu.roll(running, 1, 0), 1.0)
    for k in range(3):
        after = after * jnp.where(block < BLOCKS - 2**k, pltpu.roll(after, BLOCKS - 2**k, 0), 1.0)
        ahead = ahead * jnp.where(block >= 2**k, pltpu.roll(ahead, 2**k, 0), 1.0)

    at_re, at_im = jnp.ones_like(power_re), jnp.zeros_like(power_re)
    for step in range(STEPS):
        power_ref[32 * step : 32 * step + 16, :] = at_re
        power_ref[32 * step + 16 : 32 * step + 32, :] = at_im
        at_re, at_im = cmul(at_re, at_im, power_re, power_im)

    def wide(place):
        return jnp.broadcast_to(pack_ref[place : place + 1, lanes], (BLOCKS, HALF))

    for h in range(2):
        lanes = slice(HALF * h, HALF * h + HALF)
        for j in range(NDIM):
            out_re, out_im = after, jnp.zeros_like(after)
            in_re, in_im = cmul(ahead * wide(32 + j), ahead * wide(48 + j), wide(j), wide(16 + j))
            for k in range(3):
                far_re, far_im = wide(64 + 32 * k + j), wide(80 + 32 * k + j)
                chosen = (block // 2**k) % 2 == 1
                on_re, on_im = cmul(in_re, in_im, far_re, far_im)
                in_re, in_im = jnp.where(chosen, on_re, in_re), jnp.where(chosen, on_im, in_im)
                on_re, on_im = cmul(out_re, out_im, far_re, far_im)
                out_re, out_im = jnp.where(chosen, out_re, on_re), jnp.where(chosen, out_im, on_im)
            leave_ref[16 * j : 16 * j + 8, lanes] = out_re
            leave_ref[16 * j + 8 : 16 * j + 16, lanes] = out_im
            enter_ref[16 * j : 16 * j + 8, lanes] = in_re
            enter_ref[16 * j + 8 : 16 * j + 16, lanes] = in_im


def local_kernel(
    stats_ref,
    sums_ref,
    squares_ref,
    placed_ref,
    back_ref,
    pack_ref,
    leave_ref,
    power_ref,
    message_ref,
    scaled_ref,
    ends_ref,
    summary,
):
    me = lax.axis_index("span")
    before = jnp.zeros((8, WIDTH), f32)
    for i in range(SPANS):
        before += jnp.where(i < me, stats_ref[8 * i : 8 * i + 8, :], 0.0)

    before = dot_parts(before, group_matrix())
    cum_sum = sums_ref[...] + before[0:1]
    cum_sq = squares_ref[...] + before[1:2]
    position = time_of(iota2((LENGTH, WIDTH), 0)) + me * LENGTH + 1
    share = 1.0 / (position * GROUP).astype(f32)
    average = cum_sum * share
    spread = cum_sq * share - average * average
    inverse = lax.rsqrt(spread + norm_eps)
    normed = (placed_ref[...] - average) * inverse * pack_ref[200:201, :] + pack_ref[208:209, :]
    back = back_ref[...]
    scaled_ref[...] = normed * jnp.concatenate([back, back], axis=1)

    for h in range(2):
        lanes = slice(HALF * h, HALF * h + HALF)
        for first in range(0, NDIM, CHUNK):

            u = scaled_ref[LENGTH - BLOCKS : LENGTH, lanes]
            ends = [u] * CHUNK + [u * 0.0] * CHUNK
            for step in range(1, STEPS):
                row = LENGTH - BLOCKS * (step + 1)
                u = scaled_ref[row : row + BLOCKS, lanes]
                for n in range(2 * CHUNK):
                    place = 32 * step + 16 * (n // CHUNK) + first + n % CHUNK
                    ends[n] = ends[n] + u * power_ref[place : place + 1, lanes]
            for n in range(CHUNK):
                j = first + n
                ends_ref[16 * j : 16 * j + 8, lanes] = ends[n]
                ends_ref[16 * j + 8 : 16 * j + 16, lanes] = ends[CHUNK + n]
                end_re, end_im = cmul(
                    ends[n],
                    ends[CHUNK + n],
                    leave_ref[16 * j : 16 * j + 8, lanes],
                    leave_ref[16 * j + 8 : 16 * j + 16, lanes],
                )
                summary[j : j + 1, lanes] = jnp.sum(end_re, axis=0, keepdims=True)
                summary[16 + j : 17 + j, lanes] = jnp.sum(end_im, axis=0, keepdims=True)
    sent = summary[...].astype(bf16)
    for i in range(SPANS):
        message_ref[32 * i : 32 * i + 32, :] = sent


def within_kernel(scaled_ref, ends_ref, retained_ref, pack_ref, mixed):
    block = iota2((BLOCKS, HALF), 0)
    running = retained_ref[LENGTH - BLOCKS : LENGTH, :]
    spans = [running]
    for k in range(2):
        reach = spans[-1]
        shifted = jnp.where(block >= 2**k, pltpu.roll(reach, 2**k, 0), 1.0)
        spans.append(reach * shifted)
    spans = [jnp.where(block >= 2**k, spans[k], 0.0) for k in range(3)]

    def wide(place, lanes):
        return jnp.broadcast_to(pack_ref[place : place + 1, lanes], (BLOCKS, HALF))

    for h in range(2):
        lanes = slice(HALF * h, HALF * h + HALF)
        for first in range(0, NDIM, CHUNK):
            js = range(first, first + CHUNK)
            re_of = [wide(j, lanes) for j in js]
            im_of = [wide(16 + j, lanes) for j in js]

            begin = []
            for n, j in enumerate(js):
                re = running * ends_ref[16 * j : 16 * j + 8, lanes]
                im = running * ends_ref[16 * j + 8 : 16 * j + 16, lanes]
                for k in range(3):
                    add_re, add_im = cmul(
                        pltpu.roll(re, 2**k, 0),
                        pltpu.roll(im, 2**k, 0),
                        wide(64 + 32 * k + j, lanes),
                        wide(80 + 32 * k + j, lanes),
                    )
                    re, im = re + spans[k] * add_re, im + spans[k] * add_im
                begin.append(jnp.where(block >= 1, pltpu.roll(re, 1, 0), 0.0))
                begin.append(jnp.where(block >= 1, pltpu.roll(im, 1, 0), 0.0))
            out_re = [wide(32 + j, lanes) for j in js]
            out_im = [wide(48 + j, lanes) for j in js]
            skip = pack_ref[192:200, lanes]

            def step_on(step, held):
                rows = pl.ds(pl.multiple_of(step * BLOCKS, BLOCKS), BLOCKS)
                u = scaled_ref[rows, lanes]
                following = []
                terms = []
                for n in range(CHUNK):
                    re, im = held[2 * n], held[2 * n + 1]
                    next_re = re * re_of[n] - im * im_of[n] + u
                    next_im = re * im_of[n] + im * re_of[n]
                    following += [next_re, next_im]
                    terms.append(out_re[n] * next_re - out_im[n] * next_im)
                while len(terms) > 1:
                    terms = [terms[i] + terms[i + 1] for i in range(0, len(terms), 2)]
                if first == 0:
                    mixed[rows, lanes] = terms[0] + skip * u
                else:
                    mixed[rows, lanes] += terms[0]
                return tuple(following)

            lax.fori_loop(0, STEPS, step_on, tuple(begin), unroll=2)


def finish_kernel(
    message_ref,
    stats_ref,
    mixed_ref,
    retained_ref,
    pack_ref,
    enter_ref,
    power_ref,
    weight_ref,
    give_ref,
    keep_ref,
    entering,
    mixed,
):
    me = lax.axis_index("span")
    core = lax.axis_index("tensor") % 2
    far_re, far_im = pack_ref[160:176, :], pack_ref[176:192, :]

    def turn(i, held):
        kept = stats_ref[pl.ds(i * 8 + 2, 1), :]
        piece = message_ref[pl.ds(pl.multiple_of(i * 32, 32), 32), :].astype(f32)
        re, im = cmul(held[0], held[1], far_re, far_im)
        return re * kept + piece[:16], im * kept + piece[16:]

    start = jnp.zeros((NDIM, WIDTH), f32)
    state_re, state_im = lax.fori_loop(0, me, turn, (start, start))
    entering[0:16, :] = state_re
    entering[16:32, :] = state_im

    for h in range(2):
        lanes = slice(HALF * h, HALF * h + HALF)
        for first in range(0, NDIM, CHUNK):
            held = []
            for j in range(first, first + CHUNK):
                held.append(
                    cmul(
                        jnp.broadcast_to(entering[j : j + 1, lanes], (BLOCKS, HALF)),
                        jnp.broadcast_to(entering[16 + j : 17 + j, lanes], (BLOCKS, HALF)),
                        enter_ref[16 * j : 16 * j + 8, lanes],
                        enter_ref[16 * j + 8 : 16 * j + 16, lanes],
                    )
                )
            for step in range(STEPS):
                rows = slice(BLOCKS * step, BLOCKS * step + BLOCKS)
                terms = [
                    re * power_ref[32 * step + first + n : 32 * step + first + n + 1, lanes]
                    - im * power_ref[32 * step + 16 + first + n : 32 * step + 17 + first + n, lanes]
                    for n, (re, im) in enumerate(held)
                ]
                while len(terms) > 1:
                    terms = [terms[i] + terms[i + 1] for i in range(0, len(terms), 2)]
                so_far = mixed_ref[rows, lanes] if first == 0 else mixed[rows, lanes]
                mixed[rows, lanes] = so_far + terms[0]

    retained = retained_ref[...]
    ema = jnp.concatenate([retained, retained], axis=1) * mixed[...]
    active = (ema / (1.0 + jnp.exp(-ema))).astype(bf16)
    slot = iota2((LENGTH, LENGTH), 0)
    wanted = (slot + (1 - core) * HALF) % LENGTH
    chosen = as_bf16(time_of(iota2((LENGTH, LENGTH), 1)) == wanted)
    ordered = dot(chosen, active).astype(bf16)
    product = dot(ordered, weight_ref[...]).astype(bf16)
    give_ref[...] = product[:HALF]
    keep_ref[...] = product[HALF:]


def norm_kernel(parts_ref, gain_ref, out_ref):
    total = parts_ref[0:16, :].astype(f32)
    for i in range(1, 8):
        total += parts_ref[16 * i : 16 * i + 16, :].astype(f32)
    squares = jnp.mean(total * total, axis=1, keepdims=True)
    normed = (total * lax.rsqrt(squares + scale_eps) * gain_ref[...]).astype(bf16)
    for i in range(8):
        out_ref[16 * i : 16 * i + 16, :] = normed


def half_kernel(own, shared_ref, weight_ref, *refs):
    out_ref, half, done = refs[-3:]
    core = lax.axis_index("tensor") % 2
    side = core if own else 1 - core
    place = pl.multiple_of(side * HALF, HALF)
    half[...] = dot(shared_ref[...], weight_ref[...]).astype(bf16)
    copy = pltpu.make_async_copy(half, out_ref.at[pl.ds(place, HALF), :], done)
    copy.start()
    copy.wait()


def half_call(own, *operands):
    return pl.pallas_call(
        functools.partial(half_kernel, own),
        out_shape=jax.ShapeDtypeStruct((LENGTH, WIDTH), bf16),
        in_specs=[VMEM, VMEM] + [HBM] * (len(operands) - 2),
        out_specs=HBM,
        scratch_shapes=[pltpu.VMEM((HALF, WIDTH), bf16), pltpu.SemaphoreType.DMA],
        input_output_aliases={} if own else {2: 0},
        compiler_params=pltpu.CompilerParams(vmem_limit_bytes=16 * 2**20),
        cost_estimate=pl.CostEstimate(flops=10**9, bytes_accessed=2**20, transcendentals=0),
    )(*operands)


def call(kernel, count, shapes, scratch=(), space=VMEM, limit=32, cost=None):
    single = len(shapes) == 1
    made = [jax.ShapeDtypeStruct(s, d) for s, d in shapes]
    return pl.pallas_call(
        kernel,
        out_shape=made[0] if single else made,
        in_specs=[space] * count,
        out_specs=VMEM if single else [VMEM] * len(shapes),
        scratch_shapes=list(scratch),
        compiler_params=pltpu.CompilerParams(vmem_limit_bytes=limit * 2**20),
        cost_estimate=cost,
    )


def shards(
    tokens,
    retain,
    norm_gain,
    norm_bias,
    decay_rate,
    ema_angle,
    ema_input,
    ema_output,
    ema_skip,
    shared_weight,
    shared_gain,
    output_weight,
):
    retain = retain.reshape(1, LENGTH)
    with jax.named_scope("stats"):
        own = call(
            stats_kernel,
            2,
            [((8 * SPANS, WIDTH), f32)],
            [
                pltpu.VMEM((LENGTH, WIDTH), bf16),
                pltpu.VMEM((1, LENGTH), f32),
                pltpu.SemaphoreType.DMA((5,)),
            ],
            HBM,
            60,
        )(tokens, retain)
        stats = lax.all_to_all(own, "span", 0, 0, tiled=True)
    with jax.named_scope("local"):
        sums, squares, placed, retained, back, pack, leave, enter, power = call(
            prepare_kernel,
            9,
            [((LENGTH, WIDTH), f32)] * 3
            + [((LENGTH, HALF), f32)] * 2
            + [((216, WIDTH), f32)]
            + [((2 * NDIM * BLOCKS, WIDTH), f32)] * 2
            + [((2 * NDIM * STEPS, WIDTH), f32)],
            limit=16,
            cost=pl.CostEstimate(flops=2 * 10**9, bytes_accessed=2**22, transcendentals=0),
        )(
            tokens,
            retain,
            decay_rate,
            ema_angle,
            ema_input,
            ema_output,
            ema_skip.reshape(1, WIDTH),
            norm_gain.reshape(1, WIDTH),
            norm_bias.reshape(1, WIDTH),
        )
        message, scaled, ends = call(
            local_kernel,
            8,
            [
                ((32 * SPANS, WIDTH), bf16),
                ((LENGTH, WIDTH), f32),
                ((2 * NDIM * BLOCKS, WIDTH), f32),
            ],
            [pltpu.VMEM((32, WIDTH), f32)],
            limit=16,
        )(stats, sums, squares, placed, back, pack, leave, power)
        message = lax.all_to_all(message, "span", 0, 0, tiled=True)
        mixed = call(
            within_kernel,
            4,
            [((LENGTH, WIDTH), f32)],
            limit=16,
            cost=pl.CostEstimate(flops=2 * 10**9, bytes_accessed=2**22, transcendentals=0),
        )(scaled, ends, retained, pack)
    with jax.named_scope("finish"):
        width = shared_weight.shape[1]
        give, keep = call(
            finish_kernel,
            8,
            [((HALF, width), bf16), ((HALF, width), bf16)],
            [pltpu.VMEM((32, WIDTH), f32), pltpu.VMEM((LENGTH, WIDTH), f32)],
            limit=16,
        )(message, stats, mixed, retained, pack, enter, power, shared_weight)
    with jax.named_scope("shared"):
        swap = [(i, i ^ 1) for i in range(16)]
        taken = lax.ppermute(give, "tensor", swap)
        pair = (taken.astype(f32) + keep.astype(f32)).astype(bf16)
        groups = [[core + 2 * z for z in range(8)] for core in range(2)]
        parts = lax.all_to_all(pair, "tensor", 0, 0, tiled=True, axis_index_groups=groups)
        copies = call(norm_kernel, 2, [((HALF, width), bf16)])(parts, shared_gain.reshape(1, width))
    with jax.named_scope("output"):
        half = lax.all_to_all(copies, "tensor", 0, 0, tiled=True, axis_index_groups=groups)
        other = lax.ppermute(half, "tensor", swap)
        out = half_call(True, half, output_weight)
        return half_call(False, other, output_weight, out)


def solution(mesh):
    in_specs = (
        P("span", "tensor"),
        P("span"),
        P("tensor"),
        P("tensor"),
        P(None, "tensor"),
        P(None, "tensor"),
        P(None, "tensor"),
        P(None, None, "tensor"),
        P("tensor"),
        P("tensor", None),
        P(),
        P(None, "tensor"),
    )
    out_specs = P("span", "tensor")
    return jax.shard_map(shards, mesh=mesh, in_specs=in_specs, out_specs=out_specs, check_vma=False)
```
